256 devices in a mesh: user: 32 (over z, y_lo, core), item: 8 (over y_hi, x).
Axes of the slice: x: 4, y: 4 (y_hi: 2, y_lo: 2; y = y_hi * 2 + y_lo), z: 8, core: 2. Of those that a mesh axis runs over, the one named last changes fastest.
Arguments:
- user_factors: bfloat16 [32768, 128], P('user'), may hold values from -1.796875 to 1.796875
- item_factors: bfloat16 [8192, 128], P('item'), may hold values from -1.796875 to 1.796875
- block_user: int32 [32, 8, 128], P('user', 'item'), may hold values from 0 to 255
- block_item: int32 [32, 8, 128], P('user', 'item'), may hold values from 0 to 7
- live_blocks: int32 [32, 8], P('user', 'item'), may hold values from 16 to 128, as said below
- ratings: int32 [32, 8, 128, 128, 128], P('user', 'item'), may hold values from 0 to 5
Outputs:
- new_users: float32 [32768, 128], P('user')
- new_items: float32 [8192, 128], P('item')
The draws below stay inside these ranges and needn't reach their ends.
Inputs may be any that keep to these rules, and one draw needn't show every extreme that they name: `live_blocks`: one device uses all 128 slots in every draw.
All inputs are finite; a program needn't handle non-finite values.
Results may differ from the reference program's by a relative error of at most 0.00091.
Values may be sent and summed in bfloat16 or wider, within the bound.
A program may use at most 128 MiB of HBM per device.

```python
import jax
import jax.numpy as jnp
from jax import lax

RANK = 128
BLK = 128
IB_DEV = 8
NB = 128
NUB = 256
NU = 32768
NI = 8192
N_USER = 32
N_ITEM = 8


def draw_live_blocks(key, part):
    key = jax.random.fold_in(key, 11)
    first_key, second_key = jax.random.split(key)
    counts = jax.random.randint(first_key, (N_USER * N_ITEM,), max(1, NB // 8), NB // 2 + 1)
    busiest = jax.random.randint(second_key, (), 0, N_USER * N_ITEM)
    filled = jnp.where(jnp.arange(N_USER * N_ITEM) == busiest, NB, counts)
    return filled.reshape(N_USER, N_ITEM).astype(jnp.int32)


def touch_ends(drawn, stream_key, least, largest):
    index_at = [jax.random.randint(jax.random.fold_in(stream_key, axis), (), 0, length) for axis, length in enumerate(drawn.shape)]
    widest = drawn.shape.index(max(drawn.shape))
    beside = index_at[:widest] + [(index_at[widest] + 1) % drawn.shape[widest]] + index_at[widest + 1:]
    return drawn.at[tuple(index_at)].set(least).at[tuple(beside)].set(largest)


def block_scale(stream_key, shape, cuts, low, high):
    factor_of, own = 1.0, jax.random.fold_in(stream_key, 6)
    for position, parts in cuts:
        steps = jnp.exp(jax.random.uniform(jax.random.fold_in(own, position), (parts,), jnp.float32, low / len(cuts), high / len(cuts)))
        factor_of = factor_of * jnp.repeat(steps, shape[position] // parts).reshape([-1 if axis == position else 1 for axis in range(len(shape))])
    return factor_of


def scatter_about(rng, shape, spread, bound, cuts=(), held_as=jnp.bfloat16):
    array = jax.random.normal(rng, shape, jnp.float32) * spread
    if len(cuts) > 0:
        array = block_scale(rng, shape, cuts, -0.22, 0.18) * array
    return jnp.clip(array, min=-bound, max=bound).astype(held_as)


def setup_inputs(seed: int = 0) -> dict:
    key_list = jax.random.split(jax.random.key(seed), 7)
    user_factors = scatter_about(key_list[0], (NU, RANK), 0.3, 1.796875, ((0, 32),))
    item_factors = scatter_about(key_list[1], (NI, RANK), 0.3, 1.796875, ((0, 8),))
    block_user = touch_ends(jax.random.randint(key_list[2], (N_USER, N_ITEM, NB), 0, NUB), jax.random.fold_in(key_list[2], 1), 0, NUB - 1).astype(jnp.int32)
    block_item = touch_ends(jax.random.randint(key_list[3], (N_USER, N_ITEM, NB), 0, IB_DEV), jax.random.fold_in(key_list[3], 1), 0, IB_DEV - 1).astype(jnp.int32)
    live_blocks = draw_live_blocks(jax.random.fold_in(key_list[6], 71), 0)
    ratings = touch_ends(jax.random.randint(key_list[5], (N_USER, N_ITEM, NB, BLK, BLK), 0, 6), jax.random.fold_in(key_list[5], 1), 0, 5).astype(jnp.int32)
    return dict(user_factors=user_factors, item_factors=item_factors, block_user=block_user, block_item=block_item, live_blocks=live_blocks, ratings=ratings)


user_step = 0.1
item_step = 0.04
shrinkage = 0.1


def reference(user_factors, item_factors, block_user, block_item, live_blocks, ratings):
    tile_edge = ratings.shape[-1]
    slot_count = ratings.shape[2]
    factor_dim = user_factors.shape[1]
    user_tiles_all = user_factors.reshape(-1, tile_edge, factor_dim).astype(jnp.float32)
    item_tiles_all = item_factors.reshape(-1, tile_edge, factor_dim).astype(jnp.float32)
    flat_users = block_user.reshape(-1, slot_count)
    flat_items = block_item.reshape(-1, slot_count)
    flat_live = live_blocks.reshape(-1)
    flat_ratings = ratings.reshape(-1, slot_count, tile_edge, tile_edge)
    columns = jnp.arange(flat_users.shape[0], dtype=jnp.int32) % N_ITEM
    slots = jnp.arange(slot_count, dtype=jnp.int32)

    def visit(totals, record):
        user_total, item_total = totals
        user_block, item_block, live_count, scores, column = record
        global_item = (column * IB_DEV + item_block).astype(jnp.int32)
        user_tiles = user_tiles_all[user_block]
        item_tiles = item_tiles_all[global_item]
        predicted = jnp.einsum("bir,bjr->bij", user_tiles, item_tiles, precision=lax.Precision.HIGHEST)
        observed = (scores > 0) & (slots < live_count)[:, None, None]
        target = scores.astype(jnp.float32) - 3.0
        errors = jnp.where(observed, predicted - target, jnp.float32(0.0)).astype(jnp.bfloat16).astype(jnp.float32)
        user_terms = jnp.einsum("bij,bjr->bir", errors, item_tiles, precision=lax.Precision.HIGHEST)
        item_terms = jnp.einsum("bij,bir->bjr", errors, user_tiles, precision=lax.Precision.HIGHEST)
        user_total = user_total.at[user_block].add(user_terms)
        item_total = item_total.at[global_item].add(item_terms)
        return (user_total, item_total), None

    start = (jnp.zeros(user_tiles_all.shape, jnp.float32), jnp.zeros(item_tiles_all.shape, jnp.float32))
    (user_total, item_total), _ = lax.scan(visit, start, (flat_users, flat_items, flat_live, flat_ratings, columns))
    user_grad = user_total.reshape(-1, factor_dim)
    item_grad = item_total.reshape(-1, factor_dim)
    user_now = user_factors.astype(jnp.float32)
    item_now = item_factors.astype(jnp.float32)
    new_users = user_now - user_step * (user_grad + shrinkage * user_now)
    new_items = item_now - item_step * (item_grad + shrinkage * item_now)
    return new_users, new_items
```

```python
import functools

import jax
import jax.numpy as jnp
from jax import lax
from jax.experimental import pallas as pl
from jax.experimental.pallas import tpu as pltpu
from jax.sharding import PartitionSpec as P

MESH = pl.DeviceIdType.MESH


def here():
    p = lax.axis_index("user")
    q = lax.axis_index("item")
    return p // 4, lax.rem(p // 2, 2), q // 4, lax.rem(q, 4), lax.rem(p, 2)


def device(z, y, x, c):
    return (z * 4 + lax.rem(y, 2) * 2 + c, (y // 2) * 4 + x)


def neighbours():
    z, ylo, yhi, x, c = here()
    y = yhi * 2 + ylo
    up = lambda v, n: lax.rem(v + 1, n)
    down = lambda v, n: lax.rem(v + n - 1, n)
    return {
        "x": (device(z, y, up(x, 4), c), device(z, y, down(x, 4), c)),
        "y": (device(z, up(y, 4), x, c), device(z, down(y, 4), x, c)),
        "z": (device(up(z, 8), y, x, c), device(down(z, 8), y, x, c)),
        "pair": device(z, yhi * 2 + 1 - ylo, x, c),
        "mate": device(z, y, x, 1 - c),
    }


def meet(near):
    barrier = pltpu.get_barrier_semaphore()
    others = [*near["x"], *near["y"], *near["z"], near["mate"]]
    for other in others:
        pl.semaphore_signal(barrier, inc=1, device_id=other, device_id_type=MESH)
    pl.semaphore_wait(barrier, len(others))


class Sender:
    def __init__(self, send_sems, recv_sems):
        self.send_sems, self.recv_sems, self.used, self.copies = send_sems, recv_sems, 0, []

    def __call__(self, src, dst, where):
        copy = pltpu.make_async_remote_copy(
            src_ref=src,
            dst_ref=dst,
            send_sem=self.send_sems.at[self.used],
            recv_sem=self.recv_sems.at[self.used],
            device_id=where,
            device_id_type=MESH,
        )
        copy.start()
        self.used += 1
        self.copies.append(copy)
        return copy

    def drain(self):
        for copy in self.copies:
            copy.wait_send()


ROWS_A, ROWS_B, ROWS_C = 64, 32, 32
GATHER_COPIES = 160


def gather_kernel(split, own, ratings, lists, users, mate_ratings, mate_lists, local_sem, send_sems, recv_sems):
    z, ylo, yhi, x, c = here()
    y = yhi * 2 + ylo
    near = neighbours()
    keep = pltpu.make_async_copy(own, users.at[z, ylo], local_sem)
    keep.start()
    meet(near)
    send = Sender(send_sems, recv_sems)
    keep.wait()
    rows_a = pl.ds(0, split[0])
    rows_b = pl.ds(split[0], split[1])
    rows_c = pl.ds(split[0] + split[1], split[2])

    def zed(offset):
        return lax.rem(z + offset + 8, 8)

    def part_a(zz, low, xx, half=None):
        if half is None:
            return users.at[zz, low, :, xx, rows_a]
        return users.at[zz, low, half, xx, rows_a]

    def part_b(zz, yy, half=None):
        if half is None:
            return users.at[zz, lax.rem(yy, 2), yy // 2, :, rows_b]
        return users.at[zz, lax.rem(yy, 2), yy // 2, pl.ds(2 * half, 2), rows_b]

    def part_c(zz, low, half=None):
        if half is None:
            return users.at[zz, low, :, :, rows_c]
        return users.at[zz, low, half, :, rows_c]

    parts = {
        "A": lambda zz, half=None: part_a(zz, ylo, x, half),
        "B": lambda zz, half=None: part_b(zz, y, half),
        "C": lambda zz, half=None: part_c(zz, ylo, half),
        "D": lambda zz, half=None: part_c(zz, 1 - ylo, half),
    }
    along_z, pair, first, last = {}, {}, {}, []

    def z_send(name, step):
        for way in (0, 1):
            offset = -(step - 1) if way == 0 else step - 1
            block = parts[name](zed(offset), way if step == 4 else None)
            along_z[name, step, way] = send(block, block, near["z"][way])

    def z_wait(name, step):
        for way in (0, 1):
            along_z[name, step, way].wait_recv()

    def pair_send(offset):
        block = part_a(zed(offset), ylo, x)
        pair[offset] = send(block, block, near["pair"])

    def x_send(offset, low):
        if offset == 0 and low == 0:
            return
        block = part_a(zed(offset), ylo if low == 0 else 1 - ylo, x)
        first["x", offset, low] = [send(block, block, near["x"][way]) for way in (0, 1)]

    def y_send(offset):
        block = part_b(zed(offset), y)
        first["y", offset, 0] = [send(block, block, near["y"][way]) for way in (0, 1)]

    def forward(axis, offset, low):
        zz = zed(offset)
        if axis == "x" and offset == 0 and low == 0:
            return
        for way in (0, 1):
            first[axis, offset, low][way].wait_recv()
            if axis == "y" and offset == 0:
                continue
            back = 3 if way == 0 else 1
            if axis == "x":
                block = part_a(zz, ylo if low == 0 else 1 - ylo, lax.rem(x + back, 4), way)
            else:
                block = part_b(zz, lax.rem(y + back, 4), way)
            last.append(send(block, block, near[axis][way]))

    z_send("A", 1)
    z_send("B", 1)
    pair_c = send(part_c(z, ylo), part_c(z, ylo), near["pair"])
    pair_send(0)
    x_send(0, 0)
    y_send(0)
    z_send("C", 1)
    far = send(ratings, mate_ratings, near["mate"])
    far_lists = send(lists, mate_lists, near["mate"])
    before = [0]
    for step in (1, 2, 3, 4):
        offsets = [-step, step] if step < 4 else [4]
        z_wait("A", step)
        if step < 4:
            z_send("A", step + 1)
        z_wait("B", step)
        if step < 4:
            z_send("B", step + 1)
        for offset in offsets:
            pair_send(offset)
            x_send(offset, 0)
            y_send(offset)
        if step == 1:
            pair_c.wait_recv()
            z_send("D", 1)
        z_wait("C", step)
        if step < 4:
            z_send("C", step + 1)
        for offset in before:
            pair[offset].wait_recv()
            x_send(offset, 1)
        for offset in before:
            forward("y", offset, 0)
            forward("x", offset, 0)
        if step > 1:
            z_wait("D", step - 1)
            z_send("D", step)
            for offset in earlier:
                forward("x", offset, 1)
        earlier, before = before, offsets
    for offset in before:
        pair[offset].wait_recv()
        x_send(offset, 1)
    for offset in before:
        forward("y", offset, 0)
        forward("x", offset, 0)
    for offset in earlier + before:
        forward("x", offset, 1)
    z_wait("D", 4)
    for copy in last:
        copy.wait_recv()
    far.wait_recv()
    far_lists.wait_recv()
    send.drain()


def gather(user_factors, ratings, lists, vmem=True):
    space = pltpu.VMEM if vmem else pltpu.HBM
    return pl.pallas_call(
        functools.partial(gather_kernel, (ROWS_A, ROWS_B, ROWS_C)),
        out_shape=(
            jax.ShapeDtypeStruct((8, 2, 2, 4, 128, 128), jnp.bfloat16),
            jax.ShapeDtypeStruct(ratings.shape, jnp.int32),
            jax.ShapeDtypeStruct(lists.shape, jnp.int32),
        ),
        in_specs=[
            pl.BlockSpec(memory_space=space),
            pl.BlockSpec(memory_space=pltpu.HBM),
            pl.BlockSpec(memory_space=pltpu.VMEM),
        ],
        out_specs=(
            pl.BlockSpec(memory_space=space),
            pl.BlockSpec(memory_space=pltpu.HBM),
            pl.BlockSpec(memory_space=pltpu.VMEM),
        ),
        scratch_shapes=[
            pltpu.SemaphoreType.DMA,
            pltpu.SemaphoreType.DMA((GATHER_COPIES,)),
            pltpu.SemaphoreType.DMA((GATHER_COPIES,)),
        ],
        compiler_params=pltpu.CompilerParams(
            collective_id=0, has_side_effects=True, vmem_limit_bytes=40 * 2**20
        ),
    )(user_factors.reshape(2, 4, 128, 128), ratings, lists)


GROUP = 4
SLOTS = 32


def local_kernel(core, lists, mate_lists, users_hbm, items, ratings, mate_ratings, user_out, item_out, users, user_sum, item_sum, stack, order, users_sem, rating_sems, out_sems):
    load = pltpu.make_async_copy(users_hbm, users, users_sem)
    load.start()
    mine = core[0]
    edge = ratings.shape[1]

    def scan(table, base):
        def visit(slot, count):
            block = table[0, slot]
            item = table[1, slot]
            order[count] = (((base + slot) * 256 + block) * 8) + item
            keep = lax.rem(block // 8, 2) == mine
            return count + keep.astype(jnp.int32)
        return visit

    count = lax.fori_loop(0, lists[2, 0], scan(lists, 0), jnp.int32(0))
    count = lax.fori_loop(0, mate_lists[2, 0], scan(mate_lists, 128), count)
    groups = (count + GROUP - 1) // GROUP
    for k in range(GROUP):
        order[count + k] = 0

    def fetch(n, start):
        slot = order[n] // 2048
        place = lax.rem(n, SLOTS)

        @pl.when(slot < 128)
        def _():
            copy = pltpu.make_async_copy(ratings.at[slot], stack.at[place], rating_sems.at[place])
            copy.start() if start else copy.wait()

        @pl.when(slot >= 128)
        def _():
            copy = pltpu.make_async_copy(mate_ratings.at[slot - 128], stack.at[place], rating_sems.at[place])
            copy.start() if start else copy.wait()

    ahead = SLOTS - GROUP

    def begin(n, carry):
        fetch(n, True)
        return carry

    lax.fori_loop(0, jnp.minimum(groups * GROUP, ahead), begin, 0)

    def clear(k, carry):
        user_sum[k] = jnp.zeros((edge, 128), jnp.float32)
        return carry

    lax.fori_loop(0, 128, clear, 0)
    item_sum[...] = jnp.zeros_like(item_sum)
    load.wait()

    def step(g, carry):
        first = g * GROUP
        for k in range(GROUP):
            fetch(first + k, False)
        records = []
        for k in range(GROUP):
            n = first + k
            entry = order[n]
            item = lax.rem(entry, 8)
            block = lax.rem(entry // 8, 256)
            tile = (block // 16) * 8 + lax.rem(block, 8)
            user_tile = users[tile]
            item_tile = items[item]
            predicted = lax.dot_general(
                user_tile, item_tile, (((1,), (1,)), ((), ())), preferred_element_type=jnp.float32
            )
            scores = stack[lax.rem(n, SLOTS)]
            floor = jnp.where(n < count, 0, 1 << 20)
            errors = jnp.where(
                scores > floor, predicted - (scores.astype(jnp.float32) - 3.0), 0.0
            ).astype(jnp.bfloat16)
            records.append((tile, item, user_tile, item_tile, errors))
        terms = []
        for tile, item, user_tile, item_tile, errors in records:
            user_term = jnp.dot(errors, item_tile, preferred_element_type=jnp.float32)
            item_term = lax.dot_general(
                errors, user_tile, (((0,), (0,)), ((), ())), preferred_element_type=jnp.float32
            )
            terms.append((tile, item, user_term, item_term))
        for tile, item, user_term, item_term in terms:
            user_sum[tile] += user_term
            item_sum[item] += item_term
        for k in range(GROUP):
            later = first + k + ahead

            @pl.when(later < groups * GROUP)
            def _(later=later):
                fetch(later, True)

        return carry

    lax.fori_loop(0, groups, step, 0)
    outs = [
        pltpu.make_async_copy(user_sum, user_out, out_sems.at[0]),
        pltpu.make_async_copy(item_sum, item_out, out_sems.at[1]),
    ]
    for copy in outs:
        copy.start()
    for copy in outs:
        copy.wait()


def local(core, lists, mate_lists, users, items, ratings, mate_ratings):
    smem = pl.BlockSpec(memory_space=pltpu.SMEM)
    hbm = pl.BlockSpec(memory_space=pltpu.HBM)
    return pl.pallas_call(
        local_kernel,
        out_shape=(
            jax.ShapeDtypeStruct((128, 128, 128), jnp.float32),
            jax.ShapeDtypeStruct((8, 128, 128), jnp.float32),
        ),
        in_specs=[smem, smem, smem, hbm, pl.BlockSpec(memory_space=pltpu.VMEM), hbm, hbm],
        out_specs=(hbm, hbm),
        scratch_shapes=[
            pltpu.VMEM((128, 128, 128), jnp.bfloat16),
            pltpu.VMEM((128, 128, 128), jnp.float32),
            pltpu.VMEM((8, 128, 128), jnp.float32),
            pltpu.VMEM((SLOTS, 128, 128), jnp.int32),
            pltpu.SMEM((256 + GROUP,), jnp.int32),
            pltpu.SemaphoreType.DMA,
            pltpu.SemaphoreType.DMA((SLOTS,)),
            pltpu.SemaphoreType.DMA((2,)),
        ],
        compiler_params=pltpu.CompilerParams(vmem_limit_bytes=40 * 2**20),
    )(core, lists, mate_lists, users, items, ratings, mate_ratings)


user_step = 0.1
item_step = 0.04
shrinkage = 0.1
SCALE_ROWS = 16


def encode(value, buffer):
    rows = value.shape[0]
    folded = value.reshape(rows // 8, 8, 128)
    peak = jnp.maximum(jnp.max(jnp.abs(folded), axis=0), 1e-30)
    power = jnp.ceil(jnp.log2(peak))
    whole = jnp.round(folded * jnp.exp2(14.0 - power)).reshape(rows, 128)
    buffer[0:rows] = whole.astype(jnp.int32).astype(jnp.int16)
    both = jnp.concatenate([power, power], axis=0)
    buffer[rows:rows + SCALE_ROWS] = both.astype(jnp.int32).astype(jnp.int16)


def decode(buffer):
    rows = buffer.shape[0] - SCALE_ROWS
    power = buffer[rows:rows + SCALE_ROWS].astype(jnp.float32)[0:8]
    folded = buffer[0:rows].astype(jnp.float32).reshape(rows // 8, 8, 128)
    return (folded * jnp.exp2(power - 14.0)).reshape(rows, 128)


def reduce_kernel(
    sums_hbm, item_sums, own_users, own_items, new_users, new_items,
    sums, plane_out, plane_in, column_out, column_in, total, last_out, last_in, grads,
    item_in, item_half, item_out, item_z, item_pair_out, item_pair_in, item_grads,
    load_sems, plane_send, plane_recv, column_send, column_recv, last_send, last_recv,
    grad_send, grad_recv, item_send, item_recv, item_z_send, item_z_recv, item_back_send, item_back_recv,
):
    z, ylo, yhi, x, c = here()
    y = yhi * 2 + ylo
    q = yhi * 4 + x

    def turn(v, k, n):
        return lax.rem(v + k, n)

    def copy(src, dst, send_sem, recv_sem, where):
        return pltpu.make_async_remote_copy(
            src_ref=src, dst_ref=dst, send_sem=send_sem, recv_sem=recv_sem,
            device_id=where, device_id_type=MESH,
        )

    def offset_of(i):
        return 4 + (1 - 2 * lax.rem(i, 2)) * ((i + 1) // 2)

    def load_of(i):
        zz = turn(z, offset_of(i), 8)
        return pltpu.make_async_copy(sums_hbm.at[zz], sums.at[zz], load_sems.at[i])

    for i in range(8):
        load_of(i).start()

    barrier = pltpu.get_barrier_semaphore()
    others = [device(z, y, turn(x, k, 4), c) for k in (1, 2, 3)]
    others += [device(z, turn(y, k, 4), x, c) for k in (1, 2, 3)]
    others += [device(z, turn(y, 2, 4), turn(x, k, 4), c) for k in (1, 2, 3)]
    others += [device(turn(z, k, 8), y, x, c) for k in range(1, 8)]
    others += [device(z, y, x, 1 - c)]
    for other in others:
        pl.semaphore_signal(barrier, inc=1, device_id=other, device_id_type=MESH)
    pl.semaphore_wait(barrier, len(others))

    mate = device(z, y, x, 1 - c)
    pair = device(z, yhi * 2 + 1 - ylo, x, c)
    item_first = copy(item_sums.at[pl.ds((1 - c) * 4, 4)], item_in, item_send.at[0], item_recv.at[0], mate)
    item_first.start()

    def plane_where(part, k):
        return device(z, y, turn(x, k, 4), c) if part == 0 else device(z, turn(y, k, 4), x, c)

    def plane_block(part, zz, k):
        if part == 0:
            return sums[zz, :, :, turn(x, k, 4), 0:64].reshape(256, 128)
        other = turn(y, k, 4)
        return sums[zz, lax.rem(other, 2), other // 2, :, 64:128].reshape(256, 128)

    def plane_copy(part, i, k):
        return copy(
            plane_out.at[part, i, k - 1], plane_in.at[part, i, k - 1],
            plane_send.at[part, i, k - 1], plane_recv.at[part, i, k - 1], plane_where(part, k),
        )

    def plane_step(i, carry):
        zz = turn(z, offset_of(i), 8)
        load_of(i).wait()
        for k in (2, 1, 3):
            for part in (0, 1):
                encode(plane_block(part, zz, k), plane_out.at[part, i, k - 1])
                plane_copy(part, i, k).start()
        return carry

    def item_z_copy(o):
        return copy(
            item_out.at[o - 1], item_z.at[o - 1], item_z_send.at[o - 1], item_z_recv.at[o - 1],
            device(turn(z, o, 8), y, x, c),
        )

    lax.fori_loop(0, 1, plane_step, 0)
    item_first.wait_recv()
    item_half[...] = item_sums[pl.ds(c * 4, 4)].reshape(512, 128) + item_in[...].reshape(512, 128)

    def item_step_z(o, carry):
        zz = turn(z, o, 8)
        encode(item_half[pl.ds(pl.multiple_of(zz * 64, 64), 64)], item_out.at[o - 1])
        item_z_copy(o).start()
        return carry

    lax.fori_loop(1, 8, item_step_z, 0)
    lax.fori_loop(1, 8, plane_step, 0)

    def column_copy(part, i):
        return copy(
            column_out.at[part, i], column_in.at[part, i],
            column_send.at[part, i], column_recv.at[part, i],
            device(turn(z, offset_of(i), 8), y, x, c),
        )

    def plane_total(part, i):
        value = plane_block(part, turn(z, offset_of(i), 8), 0)
        for k in (1, 2, 3):
            plane_copy(part, i, k).wait_recv()
        for k in (1, 2, 3):
            value += decode(plane_in.at[part, i, k - 1])
        return value

    def column_step(i, carry):
        for part in (0, 1):
            encode(plane_total(part, i), column_out.at[part, i])
            column_copy(part, i).start()
        return carry

    lax.fori_loop(0, 1, column_step, 0)
    def item_gather(o, value):
        item_z_copy(o).wait_recv()
        return value + decode(item_z.at[o - 1])

    item_total = lax.fori_loop(
        1, 8, item_gather, item_half[pl.ds(pl.multiple_of(z * 64, 64), 64)]
    )
    item_pair_out[...] = item_total
    item_pair = copy(
        item_pair_out.at[pl.ds(pl.multiple_of((1 - ylo) * 32, 32), 32)], item_pair_in,
        item_send.at[1], item_recv.at[1], pair,
    )
    item_pair.start()
    lax.fori_loop(1, 3, column_step, 0)
    item_pair.wait_recv()
    encode(
        item_pair_out[pl.ds(pl.multiple_of(ylo * 32, 32), 32)] + item_pair_in[...],
        item_grads.at[c, z, ylo],
    )
    item_share = copy(
        item_grads.at[c, z, ylo], item_grads.at[c, z, ylo], item_send.at[2], item_recv.at[2], pair
    )
    item_share.start()
    lax.fori_loop(3, 4, column_step, 0)
    item_share.wait_recv()

    def item_back(o):
        return copy(
            item_grads.at[c, z], item_grads.at[c, z], item_back_send.at[o - 1], item_back_recv.at[o - 1],
            device(turn(z, o, 8), y, x, c),
        )

    def item_back_start(o, carry):
        item_back(o).start()
        return carry

    lax.fori_loop(1, 8, item_back_start, 0)
    lax.fori_loop(4, 7, column_step, 0)
    for part in (0, 1):
        total[part] = plane_total(part, 7)

    def item_back_wait(o, carry):
        item_back(o).wait_recv()
        return carry

    lax.fori_loop(1, 8, item_back_wait, 0)
    item_last = copy(item_grads.at[c], item_grads.at[c], item_send.at[3], item_recv.at[3], mate)
    item_last.start()

    def column_gather(i, carry):
        for part in (0, 1):
            column_copy(part, i).wait_recv()
            total[part] += decode(column_in.at[part, i])
        return carry

    lax.fori_loop(0, 7, column_gather, 0)

    def last_rows(part, k):
        if part == 0:
            other = turn(y, k, 4)
            place = lax.rem(other, 2) * 2 + other // 2
        else:
            place = turn(x, k, 4)
        return total[part, pl.ds(pl.multiple_of(place * 64, 64), 64)]

    def last_copy(part, k):
        return copy(
            last_out.at[part, k - 1], last_in.at[part, k - 1],
            last_send.at[part, k - 1], last_recv.at[part, k - 1], plane_where(1 - part, k),
        )

    for k in (2, 1, 3):
        for part in (0, 1):
            encode(last_rows(part, k), last_out.at[part, k - 1])
            last_copy(part, k).start()

    item_last.wait_recv()

    def item_finish(n, carry):
        grad = decode(item_grads.at[n // 16, lax.rem(n // 2, 8), lax.rem(n, 2)])
        rows = pl.ds(pl.multiple_of(n * 32, 32), 32)
        now = own_items[rows].astype(jnp.float32)
        new_items[rows] = now - item_step * (grad + shrinkage * now)
        return carry

    lax.fori_loop(0, 32, item_finish, 0)

    halves = []
    for part in (0, 1):
        value = last_rows(part, 0)
        for k in (1, 2, 3):
            last_copy(part, k).wait_recv()
            value += decode(last_in.at[part, k - 1])
        halves.append(value)
    encode(jnp.concatenate(halves, axis=0), grads.at[q])

    def grad_copy(m):
        other = turn(q, m, 8)
        return copy(
            grads.at[q], grads.at[q], grad_send.at[m - 1], grad_recv.at[m - 1],
            device(z, (other // 4) * 2 + ylo, lax.rem(other, 4), c),
        )

    for m in range(1, 8):
        grad_copy(m).start()

    def plane_drain(i, carry):
        for part in (0, 1):
            for k in (1, 2, 3):
                plane_copy(part, i, k).wait_send()
        return carry

    def column_drain(i, carry):
        for part in (0, 1):
            column_copy(part, i).wait_send()
        item_z_copy(i + 1).wait_send()
        item_back(i + 1).wait_send()
        return carry

    lax.fori_loop(0, 8, plane_drain, 0)
    lax.fori_loop(0, 7, column_drain, 0)
    for part in (0, 1):
        for k in (1, 2, 3):
            last_copy(part, k).wait_send()
    for early in (item_first, item_pair, item_share, item_last):
        early.wait_send()

    for m in range(1, 8):
        grad_copy(m).wait_recv()

    def user_finish(j, carry):
        grad = decode(grads.at[j])
        rows = pl.ds(pl.multiple_of(j * 128, 128), 128)
        now = own_users[rows].astype(jnp.float32)
        new_users[rows] = now - user_step * (grad + shrinkage * now)
        return carry

    lax.fori_loop(0, 8, user_finish, 0)
    for m in range(1, 8):
        grad_copy(m).wait_send()


def reduce(sums, item_sums, own_users, own_items):
    vmem = pl.BlockSpec(memory_space=pltpu.VMEM)
    dma = pltpu.SemaphoreType.DMA
    i16, f32 = jnp.int16, jnp.float32
    plane = (2, 8, 3, 256 + SCALE_ROWS, 128)
    column = (2, 7, 256 + SCALE_ROWS, 128)
    last = (2, 3, 64 + SCALE_ROWS, 128)
    return pl.pallas_call(
        reduce_kernel,
        out_shape=(
            jax.ShapeDtypeStruct((1024, 128), f32),
            jax.ShapeDtypeStruct((1024, 128), f32),
        ),
        in_specs=[pl.BlockSpec(memory_space=pltpu.HBM), vmem, vmem, vmem],
        out_specs=(vmem, vmem),
        scratch_shapes=[
            pltpu.VMEM((8, 2, 2, 4, 128, 128), f32),
            pltpu.VMEM(plane, i16), pltpu.VMEM(plane, i16),
            pltpu.VMEM(column, i16), pltpu.VMEM(column, i16),
            pltpu.VMEM((2, 256, 128), f32),
            pltpu.VMEM(last, i16), pltpu.VMEM(last, i16),
            pltpu.VMEM((8, 128 + SCALE_ROWS, 128), i16),
            pltpu.VMEM((4, 128, 128), f32), pltpu.VMEM((512, 128), f32),
            pltpu.VMEM((7, 64 + SCALE_ROWS, 128), i16), pltpu.VMEM((7, 64 + SCALE_ROWS, 128), i16),
            pltpu.VMEM((64, 128), f32), pltpu.VMEM((32, 128), f32),
            pltpu.VMEM((2, 8, 2, 32 + SCALE_ROWS, 128), i16),
            dma((8,)), dma((2, 8, 3)), dma((2, 8, 3)), dma((2, 7)), dma((2, 7)),
            dma((2, 3)), dma((2, 3)), dma((7,)), dma((7,)),
            dma((4,)), dma((4,)), dma((7,)), dma((7,)), dma((7,)), dma((7,)),
        ],
        compiler_params=pltpu.CompilerParams(
            collective_id=1, has_side_effects=True, vmem_limit_bytes=40 * 2**20
        ),
    )(sums.reshape(8, 2, 2, 4, 128, 128), item_sums, own_users, own_items)


def body(user_factors, item_factors, block_user, block_item, live_blocks, ratings):
    slots = ratings.shape[2]
    scores = ratings.reshape(slots, 128, 128)
    lists = jnp.concatenate(
        [
            block_user.reshape(1, slots),
            block_item.reshape(1, slots),
            jnp.broadcast_to(live_blocks.reshape(1, 1), (1, slots)),
            jnp.zeros((5, slots), jnp.int32),
        ],
        axis=0,
    )
    users, mate_scores, mate_lists = gather(user_factors, scores, lists)
    core = lax.rem(lax.axis_index("user"), 2).astype(jnp.int32).reshape(1)
    user_sums, item_sums = local(
        core, lists, mate_lists, users.reshape(128, 128, 128), item_factors.reshape(8, 128, 128),
        scores, mate_scores,
    )
    return reduce(user_sums, item_sums, user_factors, item_factors)


def solution(mesh):
    return jax.shard_map(
        body,
        mesh=mesh,
        in_specs=(
            P("user", None),
            P("item", None),
            P("user", "item", None),
            P("user", "item", None),
            P("user", "item"),
            P("user", "item", None, None, None),
        ),
        out_specs=(P("user", None), P("item", None)),
        check_vma=False,
    )
```

```python
import functools

import jax
import jax.numpy as jnp
from jax import lax
from jax.experimental import pallas as pl
from jax.experimental.pallas import tpu as pltpu
from jax.sharding import PartitionSpec as P

MESH = pl.DeviceIdType.MESH


def here():
    p = lax.axis_index("user")
    q = lax.axis_index("item")
    return p // 4, lax.rem(p // 2, 2), q // 4, lax.rem(q, 4), lax.rem(p, 2)


def device(z, y, x, c):
    return (z * 4 + lax.rem(y, 2) * 2 + c, (y // 2) * 4 + x)


def neighbours():
    z, ylo, yhi, x, c = here()
    y = yhi * 2 + ylo
    up = lambda v, n: lax.rem(v + 1, n)
    down = lambda v, n: lax.rem(v + n - 1, n)
    return {
        "x": (device(z, y, up(x, 4), c), device(z, y, down(x, 4), c)),
        "y": (device(z, up(y, 4), x, c), device(z, down(y, 4), x, c)),
        "z": (device(up(z, 8), y, x, c), device(down(z, 8), y, x, c)),
        "pair": device(z, yhi * 2 + 1 - ylo, x, c),
        "mate": device(z, y, x, 1 - c),
    }


def meet(near):
    barrier = pltpu.get_barrier_semaphore()
    others = [*near["x"], *near["y"], *near["z"], near["mate"]]
    for other in others:
        pl.semaphore_signal(barrier, inc=1, device_id=other, device_id_type=MESH)
    pl.semaphore_wait(barrier, len(others))


class Sender:
    def __init__(self, send_sems, recv_sems):
        self.send_sems, self.recv_sems, self.used, self.copies = send_sems, recv_sems, 0, []

    def __call__(self, src, dst, where):
        copy = pltpu.make_async_remote_copy(
            src_ref=src,
            dst_ref=dst,
            send_sem=self.send_sems.at[self.used],
            recv_sem=self.recv_sems.at[self.used],
            device_id=where,
            device_id_type=MESH,
        )
        copy.start()
        self.used += 1
        self.copies.append(copy)
        return copy

    def drain(self):
        for copy in self.copies:
            copy.wait_send()


ROWS_A, ROWS_B, ROWS_C = 64, 32, 32
GATHER_COPIES = 160


def gather_kernel(split, own, ratings, lists, users, all_ratings, all_lists, local_sems, send_sems, recv_sems):
    z, ylo, yhi, x, c = here()
    y = yhi * 2 + ylo
    near = neighbours()
    keep = pltpu.make_async_copy(own, users.at[z, ylo], local_sems.at[0])
    keep.start()
    near_lists = pltpu.make_async_copy(lists, all_lists.at[c], local_sems.at[1])
    near_lists.start()
    near_ratings = pltpu.make_async_copy(ratings, all_ratings.at[c], local_sems.at[2])
    near_ratings.start()
    meet(near)
    send = Sender(send_sems, recv_sems)
    keep.wait()
    rows_a = pl.ds(0, split[0])
    rows_b = pl.ds(split[0], split[1])
    rows_c = pl.ds(split[0] + split[1], split[2])

    def zed(offset):
        return lax.rem(z + offset + 8, 8)

    def part_a(zz, low, xx, half=None):
        if half is None:
            return users.at[zz, low, :, xx, rows_a]
        return users.at[zz, low, half, xx, rows_a]

    def part_b(zz, yy, half=None):
        if half is None:
            return users.at[zz, lax.rem(yy, 2), yy // 2, :, rows_b]
        return users.at[zz, lax.rem(yy, 2), yy // 2, pl.ds(2 * half, 2), rows_b]

    def part_c(zz, low, half=None):
        if half is None:
            return users.at[zz, low, :, :, rows_c]
        return users.at[zz, low, half, :, rows_c]

    parts = {
        "A": lambda zz, half=None: part_a(zz, ylo, x, half),
        "B": lambda zz, half=None: part_b(zz, y, half),
        "C": lambda zz, half=None: part_c(zz, ylo, half),
        "D": lambda zz, half=None: part_c(zz, 1 - ylo, half),
    }
    along_z, pair, first, last = {}, {}, {}, []

    def z_send(name, step):
        for way in (0, 1):
            offset = -(step - 1) if way == 0 else step - 1
            block = parts[name](zed(offset), way if step == 4 else None)
            along_z[name, step, way] = send(block, block, near["z"][way])

    def z_wait(name, step):
        for way in (0, 1):
            along_z[name, step, way].wait_recv()

    def pair_send(offset):
        block = part_a(zed(offset), ylo, x)
        pair[offset] = send(block, block, near["pair"])

    def x_send(offset, low):
        if offset == 0 and low == 0:
            return
        block = part_a(zed(offset), ylo if low == 0 else 1 - ylo, x)
        first["x", offset, low] = [send(block, block, near["x"][way]) for way in (0, 1)]

    def y_send(offset):
        block = part_b(zed(offset), y)
        first["y", offset, 0] = [send(block, block, near["y"][way]) for way in (0, 1)]

    def forward(axis, offset, low):
        zz = zed(offset)
        if axis == "x" and offset == 0 and low == 0:
            return
        for way in (0, 1):
            first[axis, offset, low][way].wait_recv()
            if axis == "y" and offset == 0:
                continue
            back = 3 if way == 0 else 1
            if axis == "x":
                block = part_a(zz, ylo if low == 0 else 1 - ylo, lax.rem(x + back, 4), way)
            else:
                block = part_b(zz, lax.rem(y + back, 4), way)
            last.append(send(block, block, near[axis][way]))

    z_send("A", 1)
    z_send("B", 1)
    pair_c = send(part_c(z, ylo), part_c(z, ylo), near["pair"])
    pair_send(0)
    x_send(0, 0)
    y_send(0)
    z_send("C", 1)
    far = send(ratings, all_ratings.at[c], near["mate"])
    far_lists = send(lists, all_lists.at[c], near["mate"])
    before = [0]
    for step in (1, 2, 3, 4):
        offsets = [-step, step] if step < 4 else [4]
        z_wait("A", step)
        if step < 4:
            z_send("A", step + 1)
        z_wait("B", step)
        if step < 4:
            z_send("B", step + 1)
        for offset in offsets:
            pair_send(offset)
            x_send(offset, 0)
            y_send(offset)
        if step == 1:
            pair_c.wait_recv()
            z_send("D", 1)
        z_wait("C", step)
        if step < 4:
            z_send("C", step + 1)
        for offset in before:
            pair[offset].wait_recv()
            x_send(offset, 1)
        for offset in before:
            forward("y", offset, 0)
            forward("x", offset, 0)
        if step > 1:
            z_wait("D", step - 1)
            z_send("D", step)
            for offset in earlier:
                forward("x", offset, 1)
        earlier, before = before, offsets
    for offset in before:
        pair[offset].wait_recv()
        x_send(offset, 1)
    for offset in before:
        forward("y", offset, 0)
        forward("x", offset, 0)
    for offset in earlier + before:
        forward("x", offset, 1)
    z_wait("D", 4)
    for copy in last:
        copy.wait_recv()
    near_lists.wait()
    near_ratings.wait()
    far.wait_recv()
    far_lists.wait_recv()
    send.drain()


def gather(user_factors, ratings, lists, vmem=True):
    space = pltpu.VMEM if vmem else pl.ANY
    return pl.pallas_call(
        functools.partial(gather_kernel, (ROWS_A, ROWS_B, ROWS_C)),
        out_shape=(
            jax.ShapeDtypeStruct((8, 2, 2, 4, 128, 128), jnp.bfloat16),
            jax.ShapeDtypeStruct((2, *ratings.shape), jnp.int32),
            jax.ShapeDtypeStruct((2, *lists.shape), jnp.int32),
        ),
        in_specs=[
            pl.BlockSpec(memory_space=pltpu.HBM),
            pl.BlockSpec(memory_space=pltpu.HBM),
            pl.BlockSpec(memory_space=pltpu.VMEM),
        ],
        out_specs=(
            pl.BlockSpec(memory_space=space),
            pl.BlockSpec(memory_space=space),
            pl.BlockSpec(memory_space=pltpu.VMEM),
        ),
        scratch_shapes=[
            pltpu.SemaphoreType.DMA((3,)),
            pltpu.SemaphoreType.DMA((GATHER_COPIES,)),
            pltpu.SemaphoreType.DMA((GATHER_COPIES,)),
        ],
        compiler_params=pltpu.CompilerParams(
            collective_id=0, has_side_effects=True, vmem_limit_bytes=8 * 2**20
        ),
    )(
        pltpu.with_memory_space_constraint(user_factors.reshape(2, 4, 128, 128), pltpu.HBM),
        pltpu.with_memory_space_constraint(ratings, pltpu.HBM),
        lists,
    )


GROUP = 16


def local_kernel(core, lists, users, items, ratings, user_sum, item_sum, order):
    mine = core[0]
    edge = ratings.shape[1]

    def scan(table):
        def visit(slot, count):
            block = lists[table, 0, slot]
            order[count] = ((table * 128 + slot) * 256 + block) * 8 + lists[table, 1, slot]
            keep = lax.rem(block // 8, 2) == mine
            return count + keep.astype(jnp.int32)
        return visit

    count = lax.fori_loop(0, lists[0, 2, 0], scan(0), jnp.int32(0))
    count = lax.fori_loop(0, lists[1, 2, 0], scan(1), count)
    for k in range(GROUP):
        order[count + k] = 0

    def clear(k, carry):
        user_sum[k] = jnp.zeros((edge, 128), jnp.float32)
        return carry

    lax.fori_loop(0, 128, clear, 0)
    item_sum[...] = jnp.zeros_like(item_sum)

    def step(g, carry):
        first = g * GROUP
        records = []
        for k in range(GROUP):
            n = first + k
            entry = order[n]
            item = lax.rem(entry, 8)
            block = lax.rem(entry // 8, 256)
            tile = (block // 16) * 8 + lax.rem(block, 8)
            user_tile = users[tile]
            item_tile = items[item]
            predicted = lax.dot_general(
                user_tile, item_tile, (((1,), (1,)), ((), ())), preferred_element_type=jnp.float32
            )
            scores = ratings[entry // 2048]
            floor = jnp.where(n < count, 0, 1 << 20)
            errors = jnp.where(
                scores > floor, predicted - (scores.astype(jnp.float32) - 3.0), 0.0
            ).astype(jnp.bfloat16)
            records.append((tile, item, user_tile, item_tile, errors))
        terms = []
        for tile, item, user_tile, item_tile, errors in records:
            user_term = jnp.dot(errors, item_tile, preferred_element_type=jnp.float32)
            item_term = lax.dot_general(
                errors, user_tile, (((0,), (0,)), ((), ())), preferred_element_type=jnp.float32
            )
            terms.append((tile, item, user_term, item_term))
        for tile, item, user_term, item_term in terms:
            user_sum[tile] += user_term
            item_sum[item] += item_term
        return carry

    lax.fori_loop(0, (count + GROUP - 1) // GROUP, step, 0)


def local(core, lists, users, items, ratings):
    smem = pl.BlockSpec(memory_space=pltpu.SMEM)
    vmem = pl.BlockSpec(memory_space=pltpu.VMEM)
    return pl.pallas_call(
        local_kernel,
        out_shape=(
            jax.ShapeDtypeStruct((128, 128, 128), jnp.float32),
            jax.ShapeDtypeStruct((8, 128, 128), jnp.float32),
        ),
        in_specs=[smem, smem, vmem, vmem, vmem],
        out_specs=(vmem, vmem),
        scratch_shapes=[pltpu.SMEM((256 + GROUP,), jnp.int32)],
        compiler_params=pltpu.CompilerParams(vmem_limit_bytes=8 * 2**20),
    )(core, lists, users, items, ratings)


user_step = 0.1
item_step = 0.04
shrinkage = 0.1
SCALE_ROWS = 16


def encode(value, buffer):
    rows = value.shape[0]
    folded = value.reshape(rows // 8, 8, 128)
    peak = jnp.maximum(jnp.max(jnp.abs(folded), axis=0), 1e-30)
    power = jnp.ceil(jnp.log2(peak))
    whole = jnp.round(folded * jnp.exp2(14.0 - power)).reshape(rows, 128)
    buffer[0:rows] = whole.astype(jnp.int32).astype(jnp.int16)
    both = jnp.concatenate([power, power], axis=0)
    buffer[rows:rows + SCALE_ROWS] = both.astype(jnp.int32).astype(jnp.int16)


def decode(buffer):
    rows = buffer.shape[0] - SCALE_ROWS
    power = buffer[rows:rows + SCALE_ROWS].astype(jnp.float32)[0:8]
    folded = buffer[0:rows].astype(jnp.float32).reshape(rows // 8, 8, 128)
    return (folded * jnp.exp2(power - 14.0)).reshape(rows, 128)


def reduce_kernel(
    sums, item_sums, own_users, own_items, new_users, new_items,
    half_out, half_in, near_out, near_in, far_out, far_in, column_out, column_in, total, last_out, last_in, grads,
    item_in, item_half, item_out, item_z, item_pair_out, item_pair_in, item_grads,
    half_send, half_recv, near_send, near_recv, far_send, far_recv, column_send, column_recv, last_send, last_recv,
    grad_send, grad_recv, item_send, item_recv, item_z_send, item_z_recv, item_back_send, item_back_recv,
):
    z, ylo, yhi, x, c = here()
    y = yhi * 2 + ylo
    q = yhi * 4 + x

    def turn(v, k, n):
        return lax.rem(v + k, n)

    def copy(src, dst, send_sem, recv_sem, where):
        return pltpu.make_async_remote_copy(
            src_ref=src, dst_ref=dst, send_sem=send_sem, recv_sem=recv_sem,
            device_id=where, device_id_type=MESH,
        )

    def offset_of(i):
        return 4 + (1 - 2 * lax.rem(i, 2)) * ((i + 1) // 2)

    barrier = pltpu.get_barrier_semaphore()
    others = [device(z, y, turn(x, k, 4), c) for k in (1, 2, 3)]
    others += [device(z, turn(y, k, 4), x, c) for k in (1, 2, 3)]
    others += [device(z, turn(y, 2, 4), turn(x, k, 4), c) for k in (1, 2, 3)]
    others += [device(turn(z, k, 8), y, x, c) for k in range(1, 8)]
    others += [device(z, y, x, 1 - c)]
    for other in others:
        pl.semaphore_signal(barrier, inc=1, device_id=other, device_id_type=MESH)
    pl.semaphore_wait(barrier, len(others))

    mate = device(z, y, x, 1 - c)
    pair = device(z, yhi * 2 + 1 - ylo, x, c)
    item_first = copy(item_sums.at[pl.ds((1 - c) * 4, 4)], item_in, item_send.at[0], item_recv.at[0], mate)
    item_first.start()

    def plane_where(part, k):
        return device(z, y, turn(x, k, 4), c) if part == 0 else device(z, turn(y, k, 4), x, c)

    def plane_block(part, zz, k):
        if part == 0:
            return sums[zz, :, :, turn(x, k, 4), 0:64].reshape(256, 128)
        other = turn(y, k, 4)
        return sums[zz, lax.rem(other, 2), other // 2, :, 64:128].reshape(256, 128)

    def toward(part, way):
        return plane_where(part, 1 if way == 0 else 3)

    def half_copy(part, i, way):
        return copy(
            half_out.at[part, i, way], half_in.at[part, i, way],
            half_send.at[part, i, way], half_recv.at[part, i, way], toward(part, way),
        )

    def near_copy(part, i, way):
        return copy(
            near_out.at[part, i, way], near_in.at[part, i, way],
            near_send.at[part, i, way], near_recv.at[part, i, way], toward(part, way),
        )

    def add_half(value, way, extra):
        if way == 0:
            return jnp.concatenate([value[0:128] + extra, value[128:256]], axis=0)
        return jnp.concatenate([value[0:128], value[128:256] + extra], axis=0)

    def half_step(i, carry):
        zz = turn(z, offset_of(i), 8)
        for way in (0, 1):
            for part in (0, 1):
                block = plane_block(part, zz, 2)[128 * way:128 * way + 128]
                encode(block, half_out.at[part, i, way])
                half_copy(part, i, way).start()
        return carry

    def near_step(i, carry):
        zz = turn(z, offset_of(i), 8)
        for way in (0, 1):
            for part in (0, 1):
                half_copy(part, i, way).wait_recv()
                block = plane_block(part, zz, 1 if way == 0 else 3)
                block = add_half(block, way, decode(half_in.at[part, i, way]))
                encode(block, near_out.at[part, i, way])
                near_copy(part, i, way).start()
        return carry

    def item_z_copy(o):
        return copy(
            item_out.at[o - 1], item_z.at[o - 1], item_z_send.at[o - 1], item_z_recv.at[o - 1],
            device(turn(z, o, 8), y, x, c),
        )

    lax.fori_loop(0, 8, half_step, 0)
    item_first.wait_recv()
    item_half[...] = item_sums[pl.ds(c * 4, 4)].reshape(512, 128) + item_in[...].reshape(512, 128)

    def item_step_z(o, carry):
        zz = turn(z, o, 8)
        encode(item_half[pl.ds(pl.multiple_of(zz * 64, 64), 64)], item_out.at[o - 1])
        item_z_copy(o).start()
        return carry

    lax.fori_loop(1, 8, item_step_z, 0)
    lax.fori_loop(0, 8, near_step, 0)

    def plane_total(i):
        zz = turn(z, offset_of(i), 8)
        for part in (0, 1):
            for way in (0, 1):
                near_copy(part, i, way).wait_recv()
            value = plane_block(part, zz, 0)
            for way in (0, 1):
                value += decode(near_in.at[part, i, way])
            total[part, lax.rem(i, 2)] = value

    def z_where(way):
        return device(turn(z, 1 + 6 * way, 8), y, x, c)

    def far_copy(part, way):
        return copy(
            far_out.at[part, way], far_in.at[part, way], far_send.at[part, way], far_recv.at[part, way],
            z_where(way),
        )

    def column_copy(part, distance, way):
        return copy(
            column_out.at[part, distance - 1, way], column_in.at[part, distance - 1, way],
            column_send.at[part, distance - 1, way], column_recv.at[part, distance - 1, way],
            z_where(way),
        )

    def far_step():
        for part in (0, 1):
            for way in (0, 1):
                encode(total[part, 0, 128 * way:128 * way + 128], far_out.at[part, way])
                far_copy(part, way).start()

    def third_step(way):
        for part in (0, 1):
            far_copy(part, way).wait_recv()
            value = add_half(total[part, 1 - way], way, decode(far_in.at[part, way]))
            encode(value, column_out.at[part, 2, way])
            column_copy(part, 3, way).start()

    def column_step(i):
        way = 1 - lax.rem(i, 2)
        distance = 4 - (i + 1) // 2
        for part in (0, 1):
            column_copy(part, distance + 1, way).wait_recv()
            value = total[part, lax.rem(i, 2)] + decode(column_in.at[part, distance, way])
            encode(value, column_out.at[part, distance - 1, way])
            column_copy(part, distance, way).start()

    def both_step(i, carry):
        plane_total(i)
        column_step(i - 1)
        return carry

    plane_total(0)
    def item_gather(o, value):
        item_z_copy(o).wait_recv()
        return value + decode(item_z.at[o - 1])

    item_total = lax.fori_loop(
        1, 8, item_gather, item_half[pl.ds(pl.multiple_of(z * 64, 64), 64)]
    )
    item_pair_out[...] = item_total
    item_pair = copy(
        item_pair_out.at[pl.ds(pl.multiple_of((1 - ylo) * 32, 32), 32)], item_pair_in,
        item_send.at[1], item_recv.at[1], pair,
    )
    item_pair.start()
    plane_total(1)
    far_step()
    item_pair.wait_recv()
    encode(
        item_pair_out[pl.ds(pl.multiple_of(ylo * 32, 32), 32)] + item_pair_in[...],
        item_grads.at[c, z, ylo],
    )
    item_share = copy(
        item_grads.at[c, z, ylo], item_grads.at[c, z, ylo], item_send.at[2], item_recv.at[2], pair
    )
    item_share.start()
    plane_total(2)
    third_step(0)
    plane_total(3)
    third_step(1)
    item_share.wait_recv()

    def item_back(o):
        return copy(
            item_grads.at[c, z], item_grads.at[c, z], item_back_send.at[o - 1], item_back_recv.at[o - 1],
            device(turn(z, o, 8), y, x, c),
        )

    def item_back_start(o, carry):
        item_back(o).start()
        return carry

    lax.fori_loop(1, 8, item_back_start, 0)
    lax.fori_loop(4, 8, both_step, 0)

    def item_back_wait(o, carry):
        item_back(o).wait_recv()
        return carry

    lax.fori_loop(1, 8, item_back_wait, 0)
    item_last = copy(item_grads.at[c], item_grads.at[c], item_send.at[3], item_recv.at[3], mate)
    item_last.start()

    for part in (0, 1):
        for way in (0, 1):
            column_copy(part, 1, way).wait_recv()
            total[part, 1] += decode(column_in.at[part, 0, way])

    def last_rows(part, k):
        if part == 0:
            other = turn(y, k, 4)
            place = lax.rem(other, 2) * 2 + other // 2
        else:
            place = turn(x, k, 4)
        return total[part, 1, pl.ds(pl.multiple_of(place * 64, 64), 64)]

    def last_copy(part, k):
        return copy(
            last_out.at[part, k - 1], last_in.at[part, k - 1],
            last_send.at[part, k - 1], last_recv.at[part, k - 1], plane_where(1 - part, k),
        )

    for k in (2, 1, 3):
        for part in (0, 1):
            encode(last_rows(part, k), last_out.at[part, k - 1])
            last_copy(part, k).start()

    item_last.wait_recv()

    def item_finish(n, carry):
        grad = decode(item_grads.at[n // 16, lax.rem(n // 2, 8), lax.rem(n, 2)])
        rows = pl.ds(pl.multiple_of(n * 32, 32), 32)
        now = own_items[rows].astype(jnp.float32)
        new_items[rows] = now - item_step * (grad + shrinkage * now)
        return carry

    lax.fori_loop(0, 32, item_finish, 0)

    halves = []
    for part in (0, 1):
        value = last_rows(part, 0)
        for k in (1, 2, 3):
            last_copy(part, k).wait_recv()
            value += decode(last_in.at[part, k - 1])
        halves.append(value)
    encode(jnp.concatenate(halves, axis=0), grads.at[q])

    def grad_copy(m):
        other = turn(q, m, 8)
        return copy(
            grads.at[q], grads.at[q], grad_send.at[m - 1], grad_recv.at[m - 1],
            device(z, (other // 4) * 2 + ylo, lax.rem(other, 4), c),
        )

    for m in range(1, 8):
        grad_copy(m).start()

    def plane_drain(i, carry):
        for part in (0, 1):
            for way in (0, 1):
                half_copy(part, i, way).wait_send()
                near_copy(part, i, way).wait_send()
        return carry

    def item_drain(o, carry):
        item_z_copy(o).wait_send()
        item_back(o).wait_send()
        return carry

    lax.fori_loop(0, 8, plane_drain, 0)
    lax.fori_loop(1, 8, item_drain, 0)
    for part in (0, 1):
        for way in (0, 1):
            far_copy(part, way).wait_send()
            for distance in (1, 2, 3):
                column_copy(part, distance, way).wait_send()
    for part in (0, 1):
        for k in (1, 2, 3):
            last_copy(part, k).wait_send()
    for early in (item_first, item_pair, item_share, item_last):
        early.wait_send()

    for m in range(1, 8):
        grad_copy(m).wait_recv()

    def user_finish(j, carry):
        grad = decode(grads.at[j])
        rows = pl.ds(pl.multiple_of(j * 128, 128), 128)
        now = own_users[rows].astype(jnp.float32)
        new_users[rows] = now - user_step * (grad + shrinkage * now)
        return carry

    lax.fori_loop(0, 8, user_finish, 0)
    for m in range(1, 8):
        grad_copy(m).wait_send()


def reduce(sums, item_sums, own_users, own_items):
    vmem = pl.BlockSpec(memory_space=pltpu.VMEM)
    dma = pltpu.SemaphoreType.DMA
    i16, f32 = jnp.int16, jnp.float32
    half = (2, 8, 2, 128 + SCALE_ROWS, 128)
    near = (2, 8, 2, 256 + SCALE_ROWS, 128)
    far = (2, 2, 128 + SCALE_ROWS, 128)
    column = (2, 3, 2, 256 + SCALE_ROWS, 128)
    last = (2, 3, 64 + SCALE_ROWS, 128)
    return pl.pallas_call(
        reduce_kernel,
        out_shape=(
            jax.ShapeDtypeStruct((1024, 128), f32),
            jax.ShapeDtypeStruct((1024, 128), f32),
        ),
        in_specs=[vmem, vmem, vmem, vmem],
        out_specs=(vmem, vmem),
        scratch_shapes=[
            pltpu.VMEM(half, i16), pltpu.VMEM(half, i16),
            pltpu.VMEM(near, i16), pltpu.VMEM(near, i16),
            pltpu.VMEM(far, i16), pltpu.VMEM(far, i16),
            pltpu.VMEM(column, i16), pltpu.VMEM(column, i16),
            pltpu.VMEM((2, 2, 256, 128), f32),
            pltpu.VMEM(last, i16), pltpu.VMEM(last, i16),
            pltpu.VMEM((8, 128 + SCALE_ROWS, 128), i16),
            pltpu.VMEM((4, 128, 128), f32), pltpu.VMEM((512, 128), f32),
            pltpu.VMEM((7, 64 + SCALE_ROWS, 128), i16), pltpu.VMEM((7, 64 + SCALE_ROWS, 128), i16),
            pltpu.VMEM((64, 128), f32), pltpu.VMEM((32, 128), f32),
            pltpu.VMEM((2, 8, 2, 32 + SCALE_ROWS, 128), i16),
            dma((2, 8, 2)), dma((2, 8, 2)), dma((2, 8, 2)), dma((2, 8, 2)),
            dma((2, 2)), dma((2, 2)), dma((2, 3, 2)), dma((2, 3, 2)),
            dma((2, 3)), dma((2, 3)), dma((7,)), dma((7,)),
            dma((4,)), dma((4,)), dma((7,)), dma((7,)), dma((7,)), dma((7,)),
        ],
        compiler_params=pltpu.CompilerParams(
            collective_id=1, has_side_effects=True, vmem_limit_bytes=16 * 2**20
        ),
    )(sums.reshape(8, 2, 2, 4, 128, 128), item_sums, own_users, own_items)


def body(user_factors, item_factors, block_user, block_item, live_blocks, ratings):
    slots = ratings.shape[2]
    scores = ratings.reshape(slots, 128, 128)
    lists = jnp.concatenate(
        [
            block_user.reshape(1, slots),
            block_item.reshape(1, slots),
            jnp.broadcast_to(live_blocks.reshape(1, 1), (1, slots)),
            jnp.zeros((5, slots), jnp.int32),
        ],
        axis=0,
    )
    users, all_scores, all_lists = gather(user_factors, scores, lists)
    core = lax.rem(lax.axis_index("user"), 2).astype(jnp.int32).reshape(1)
    user_sums, item_sums = local(
        core, all_lists, users.reshape(128, 128, 128), item_factors.reshape(8, 128, 128),
        all_scores.reshape(256, 128, 128),
    )
    return reduce(user_sums, item_sums, user_factors, item_factors)


def solution(mesh):
    return jax.shard_map(
        body,
        mesh=mesh,
        in_specs=(
            P("user", None),
            P("item", None),
            P("user", "item", None),
            P("user", "item", None),
            P("user", "item"),
            P("user", "item", None, None, None),
        ),
        out_specs=(P("user", None), P("item", None)),
        check_vma=False,
    )
```

```python
import functools

import jax
import jax.numpy as jnp
from jax import lax
from jax.experimental import pallas as pl
from jax.experimental.pallas import tpu as pltpu
from jax.sharding import PartitionSpec as P

MESH = pl.DeviceIdType.MESH


def here():
    p = lax.axis_index("user")
    q = lax.axis_index("item")
    return p // 4, lax.rem(p // 2, 2), q // 4, lax.rem(q, 4), lax.rem(p, 2)


def device(z, y, x, c):
    return (z * 4 + lax.rem(y, 2) * 2 + c, (y // 2) * 4 + x)


def neighbours():
    z, ylo, yhi, x, c = here()
    y = yhi * 2 + ylo
    up = lambda v, n: lax.rem(v + 1, n)
    down = lambda v, n: lax.rem(v + n - 1, n)
    return {
        "x": (device(z, y, up(x, 4), c), device(z, y, down(x, 4), c)),
        "y": (device(z, up(y, 4), x, c), device(z, down(y, 4), x, c)),
        "z": (device(up(z, 8), y, x, c), device(down(z, 8), y, x, c)),
        "pair": device(z, yhi * 2 + 1 - ylo, x, c),
        "mate": device(z, y, x, 1 - c),
    }


def meet(near):
    barrier = pltpu.get_barrier_semaphore()
    others = [*near["x"], *near["y"], *near["z"], near["mate"]]
    for other in others:
        pl.semaphore_signal(barrier, inc=1, device_id=other, device_id_type=MESH)
    pl.semaphore_wait(barrier, len(others))


class Sender:
    def __init__(self, send_sems, recv_sems):
        self.send_sems, self.recv_sems, self.used, self.copies = send_sems, recv_sems, 0, []

    def __call__(self, src, dst, where):
        copy = pltpu.make_async_remote_copy(
            src_ref=src,
            dst_ref=dst,
            send_sem=self.send_sems.at[self.used],
            recv_sem=self.recv_sems.at[self.used],
            device_id=where,
            device_id_type=MESH,
        )
        copy.start()
        self.used += 1
        self.copies.append(copy)
        return copy

    def drain(self):
        for copy in self.copies:
            copy.wait_send()


ROWS_A, ROWS_B, ROWS_C = 48, 48, 32
GATHER_COPIES = 160


def gather_kernel(split, own, ratings, lists, users, all_ratings, all_lists, no_users, no_items, local_sems, send_sems, recv_sems):
    z, ylo, yhi, x, c = here()
    y = yhi * 2 + ylo
    near = neighbours()
    keep = pltpu.make_async_copy(own, users.at[z, ylo], local_sems.at[0])
    keep.start()
    near_lists = pltpu.make_async_copy(lists, all_lists.at[c], local_sems.at[1])
    near_lists.start()
    near_ratings = pltpu.make_async_copy(ratings, all_ratings.at[c], local_sems.at[2])
    near_ratings.start()
    meet(near)
    send = Sender(send_sems, recv_sems)
    keep.wait()
    rows_a = pl.ds(0, split[0])
    rows_b = pl.ds(split[0], split[1])
    rows_c = pl.ds(split[0] + split[1], split[2])

    def zed(offset):
        return lax.rem(z + offset + 8, 8)

    def part_a(zz, low, xx, half=None):
        if half is None:
            return users.at[zz, low, :, xx, rows_a]
        return users.at[zz, low, half, xx, rows_a]

    def part_b(zz, yy, half=None):
        if half is None:
            return users.at[zz, lax.rem(yy, 2), yy // 2, :, rows_b]
        return users.at[zz, lax.rem(yy, 2), yy // 2, pl.ds(2 * half, 2), rows_b]

    def part_c(zz, low, half=None):
        if half is None:
            return users.at[zz, low, :, :, rows_c]
        return users.at[zz, low, half, :, rows_c]

    parts = {
        "A": lambda zz, half=None: part_a(zz, ylo, x, half),
        "B": lambda zz, half=None: part_b(zz, y, half),
        "C": lambda zz, half=None: part_c(zz, ylo, half),
        "D": lambda zz, half=None: part_c(zz, 1 - ylo, half),
    }
    along_z, pair, first, last = {}, {}, {}, []

    def z_send(name, step):
        for way in (0, 1):
            offset = -(step - 1) if way == 0 else step - 1
            block = parts[name](zed(offset), way if step == 4 else None)
            along_z[name, step, way] = send(block, block, near["z"][way])

    def z_wait(name, step):
        for way in (0, 1):
            along_z[name, step, way].wait_recv()

    def pair_send(offset):
        block = part_a(zed(offset), ylo, x)
        pair[offset] = send(block, block, near["pair"])

    late = (-3, 3, 4)

    def direct(block, where):
        last.append(send(block, block, where))

    def x_send(offset, low):
        if offset == 0 and low == 0 or offset == 4 and low == 1:
            return
        if offset in late:
            block = part_a(zed(offset), ylo if low == 0 else 1 - ylo, x)
            rows = (y, yhi * 2 + 1 - ylo) if offset == 4 else (y,)
            for k in (2, 1, 3):
                for row in rows:
                    direct(block, device(z, row, lax.rem(x + k, 4), c))
            return
        block = part_a(zed(offset), ylo if low == 0 else 1 - ylo, x)
        first["x", offset, low] = [send(block, block, near["x"][way]) for way in (0, 1)]

    def y_send(offset):
        if offset in late:
            block = part_b(zed(offset), y)
            for k in (2, 1, 3):
                direct(block, device(z, lax.rem(y + k, 4), x, c))
            return
        block = part_b(zed(offset), y)
        first["y", offset, 0] = [send(block, block, near["y"][way]) for way in (0, 1)]

    def forward(axis, offset, low):
        zz = zed(offset)
        if axis == "x" and offset == 0 and low == 0 or offset in late:
            return
        for way in (0, 1):
            first[axis, offset, low][way].wait_recv()
            if axis == "y" and offset == 0:
                continue
            back = 3 if way == 0 else 1
            if axis == "x":
                block = part_a(zz, ylo if low == 0 else 1 - ylo, lax.rem(x + back, 4), way)
            else:
                block = part_b(zz, lax.rem(y + back, 4), way)
            last.append(send(block, block, near[axis][way]))

    z_send("A", 1)
    z_send("B", 1)
    pair_c = send(part_c(z, ylo), part_c(z, ylo), near["pair"])
    pair_send(0)
    z_send("C", 1)
    x_send(0, 0)
    y_send(0)
    far = send(ratings, all_ratings.at[c], near["mate"])
    far_lists = send(lists, all_lists.at[c], near["mate"])
    no_items[...] = jnp.zeros_like(no_items)

    def clear(k, carry):
        no_users[k] = jnp.zeros(no_users.shape[1:], jnp.float32)
        return carry

    lax.fori_loop(0, no_users.shape[0], clear, 0)
    before = [0]
    for step in (1, 2, 3, 4):
        offsets = [-step, step] if step < 4 else [4]
        z_wait("A", step)
        if step < 4:
            z_send("A", step + 1)
        z_wait("B", step)
        if step < 4:
            z_send("B", step + 1)
        for offset in offsets:
            pair_send(offset)
            x_send(offset, 0)
            y_send(offset)
        if step == 1:
            pair_c.wait_recv()
            z_send("D", 1)
        z_wait("C", step)
        if step < 4:
            z_send("C", step + 1)
        for offset in before:
            pair[offset].wait_recv()
            x_send(offset, 1)
        for offset in before:
            forward("y", offset, 0)
            forward("x", offset, 0)
        if step > 1:
            z_wait("D", step - 1)
            z_send("D", step)
            for offset in earlier:
                forward("x", offset, 1)
        earlier, before = before, offsets
    for offset in before:
        pair[offset].wait_recv()
        x_send(offset, 1)
    for offset in before:
        forward("y", offset, 0)
        forward("x", offset, 0)
    for offset in earlier + before:
        forward("x", offset, 1)
    z_wait("D", 4)
    for copy in last:
        copy.wait_recv()
    near_lists.wait()
    near_ratings.wait()
    far.wait_recv()
    far_lists.wait_recv()
    send.drain()


def gather(user_factors, ratings, lists, vmem=True):
    space = pltpu.VMEM if vmem else pl.ANY
    return pl.pallas_call(
        functools.partial(gather_kernel, (ROWS_A, ROWS_B, ROWS_C)),
        out_shape=(
            jax.ShapeDtypeStruct((8, 2, 2, 4, 128, 128), jnp.bfloat16),
            jax.ShapeDtypeStruct((2, *ratings.shape), jnp.int32),
            jax.ShapeDtypeStruct((2, *lists.shape), jnp.int32),
            jax.ShapeDtypeStruct((128, 128, 128), jnp.float32),
            jax.ShapeDtypeStruct((8, 128, 128), jnp.float32),
        ),
        in_specs=[
            pl.BlockSpec(memory_space=pltpu.HBM),
            pl.BlockSpec(memory_space=pltpu.HBM),
            pl.BlockSpec(memory_space=pltpu.VMEM),
        ],
        out_specs=(
            pl.BlockSpec(memory_space=space),
            pl.BlockSpec(memory_space=space),
            pl.BlockSpec(memory_space=pltpu.VMEM),
            pl.BlockSpec(memory_space=pltpu.VMEM),
            pl.BlockSpec(memory_space=pltpu.VMEM),
        ),
        scratch_shapes=[
            pltpu.SemaphoreType.DMA((3,)),
            pltpu.SemaphoreType.DMA((GATHER_COPIES,)),
            pltpu.SemaphoreType.DMA((GATHER_COPIES,)),
        ],
        compiler_params=pltpu.CompilerParams(
            collective_id=0, has_side_effects=True, vmem_limit_bytes=8 * 2**20
        ),
    )(
        pltpu.with_memory_space_constraint(user_factors.reshape(2, 4, 128, 128), pltpu.HBM),
        pltpu.with_memory_space_constraint(ratings, pltpu.HBM),
        lists,
    )


GROUP = 16


def local_kernel(core, lists, users, items, ratings, no_users, no_items, user_sum, item_sum, order):
    mine = core[0]

    def scan(table):
        def visit(slot, count):
            block = lists[table, 0, slot]
            order[count] = ((table * 128 + slot) * 256 + block) * 8 + lists[table, 1, slot]
            keep = lax.rem(block // 8, 2) == mine
            return count + keep.astype(jnp.int32)
        return visit

    count = lax.fori_loop(0, lists[0, 2, 0], scan(0), jnp.int32(0))
    count = lax.fori_loop(0, lists[1, 2, 0], scan(1), count)
    for k in range(GROUP):
        order[count + k] = 0

    def step(g, carry):
        first = g * GROUP
        records = []
        for k in range(GROUP):
            n = first + k
            entry = order[n]
            item = lax.rem(entry, 8)
            block = lax.rem(entry // 8, 256)
            tile = (block // 16) * 8 + lax.rem(block, 8)
            user_tile = users[tile]
            item_tile = items[item]
            predicted = lax.dot_general(
                user_tile, item_tile, (((1,), (1,)), ((), ())), preferred_element_type=jnp.float32
            )
            scores = ratings[entry // 2048]
            floor = jnp.where(n < count, 0, 1 << 20)
            errors = jnp.where(
                scores > floor, predicted - (scores.astype(jnp.float32) - 3.0), 0.0
            ).astype(jnp.bfloat16)
            records.append((tile, item, user_tile, item_tile, errors))
        terms = []
        for tile, item, user_tile, item_tile, errors in records:
            user_term = jnp.dot(errors, item_tile, preferred_element_type=jnp.float32)
            item_term = lax.dot_general(
                errors, user_tile, (((0,), (0,)), ((), ())), preferred_element_type=jnp.float32
            )
            terms.append((tile, item, user_term, item_term))
        for tile, item, user_term, item_term in terms:
            user_sum[tile] += user_term
            item_sum[item] += item_term
        return carry

    lax.fori_loop(0, (count + GROUP - 1) // GROUP, step, 0)


def local(core, lists, users, items, ratings, no_users, no_items):
    smem = pl.BlockSpec(memory_space=pltpu.SMEM)
    vmem = pl.BlockSpec(memory_space=pltpu.VMEM)
    return pl.pallas_call(
        local_kernel,
        out_shape=(
            jax.ShapeDtypeStruct((128, 128, 128), jnp.float32),
            jax.ShapeDtypeStruct((8, 128, 128), jnp.float32),
        ),
        in_specs=[smem, smem, vmem, vmem, vmem, vmem, vmem],
        out_specs=(vmem, vmem),
        input_output_aliases={5: 0, 6: 1},
        scratch_shapes=[pltpu.SMEM((256 + GROUP,), jnp.int32)],
        compiler_params=pltpu.CompilerParams(vmem_limit_bytes=8 * 2**20),
    )(core, lists, users, items, ratings, no_users, no_items)


user_step = 0.1
item_step = 0.04
shrinkage = 0.1
SCALE_ROWS = 16


def encode(value, buffer):
    rows = value.shape[0]
    folded = value.reshape(rows // 8, 8, 128)
    peak = jnp.maximum(jnp.max(jnp.abs(folded), axis=0), 1e-30)
    power = jnp.ceil(jnp.log2(peak))
    whole = jnp.round(folded * jnp.exp2(14.0 - power)).reshape(rows, 128)
    buffer[0:rows] = whole.astype(jnp.int32).astype(jnp.int16)
    both = jnp.concatenate([power, power], axis=0)
    buffer[rows:rows + SCALE_ROWS] = both.astype(jnp.int32).astype(jnp.int16)


def decode(buffer):
    rows = buffer.shape[0] - SCALE_ROWS
    power = buffer[rows:rows + SCALE_ROWS].astype(jnp.float32)[0:8]
    folded = buffer[0:rows].astype(jnp.float32).reshape(rows // 8, 8, 128)
    return (folded * jnp.exp2(power - 14.0)).reshape(rows, 128)


def reduce_kernel(
    sums, item_sums, own_users, own_items, new_users, new_items,
    half_out, half_in, near_out, near_in, far_out, far_in, column_out, column_in, total, last_out, last_in, grads,
    item_in, item_half, item_out, item_z, item_pair_out, item_pair_in, item_grads,
    half_send, half_recv, near_send, near_recv, far_send, far_recv, column_send, column_recv, last_send, last_recv,
    grad_send, grad_recv, item_send, item_recv, item_z_send, item_z_recv, item_back_send, item_back_recv,
):
    z, ylo, yhi, x, c = here()
    y = yhi * 2 + ylo
    q = yhi * 4 + x

    def turn(v, k, n):
        return lax.rem(v + k, n)

    def copy(src, dst, send_sem, recv_sem, where):
        return pltpu.make_async_remote_copy(
            src_ref=src, dst_ref=dst, send_sem=send_sem, recv_sem=recv_sem,
            device_id=where, device_id_type=MESH,
        )

    def offset_of(i):
        return 4 + (1 - 2 * lax.rem(i, 2)) * ((i + 1) // 2)

    barrier = pltpu.get_barrier_semaphore()
    others = [device(z, y, turn(x, k, 4), c) for k in (1, 2, 3)]
    others += [device(z, turn(y, k, 4), x, c) for k in (1, 2, 3)]
    others += [device(z, turn(y, 2, 4), turn(x, k, 4), c) for k in (1, 2, 3)]
    others += [device(turn(z, k, 8), y, x, c) for k in range(1, 8)]
    others += [device(z, y, x, 1 - c)]
    for other in others:
        pl.semaphore_signal(barrier, inc=1, device_id=other, device_id_type=MESH)
    pl.semaphore_wait(barrier, len(others))

    mate = device(z, y, x, 1 - c)
    pair = device(z, yhi * 2 + 1 - ylo, x, c)
    item_first = copy(item_sums.at[pl.ds((1 - c) * 4, 4)], item_in, item_send.at[0], item_recv.at[0], mate)
    item_first.start()

    def plane_where(part, k):
        return device(z, y, turn(x, k, 4), c) if part == 0 else device(z, turn(y, k, 4), x, c)

    def plane_block(part, zz, k):
        if part == 0:
            return sums[zz, :, :, turn(x, k, 4), 0:64].reshape(256, 128)
        other = turn(y, k, 4)
        return sums[zz, lax.rem(other, 2), other // 2, :, 64:128].reshape(256, 128)

    def toward(part, way):
        return plane_where(part, 1 if way == 0 else 3)

    def half_copy(part, i, way):
        return copy(
            half_out.at[part, i, way], half_in.at[part, i, way],
            half_send.at[part, i, way], half_recv.at[part, i, way], toward(part, way),
        )

    def near_copy(part, i, way):
        return copy(
            near_out.at[part, i, way], near_in.at[part, i, way],
            near_send.at[part, i, way], near_recv.at[part, i, way], toward(part, way),
        )

    def add_half(value, way, extra):
        if way == 0:
            return jnp.concatenate([value[0:128] + extra, value[128:256]], axis=0)
        return jnp.concatenate([value[0:128], value[128:256] + extra], axis=0)

    def half_step(i, carry):
        zz = turn(z, offset_of(i), 8)
        for way in (0, 1):
            for part in (0, 1):
                block = plane_block(part, zz, 2)[128 * way:128 * way + 128]
                encode(block, half_out.at[part, i, way])
                half_copy(part, i, way).start()
        return carry

    def near_step(i, carry):
        zz = turn(z, offset_of(i), 8)
        for way in (0, 1):
            for part in (0, 1):
                half_copy(part, i, way).wait_recv()
                block = plane_block(part, zz, 1 if way == 0 else 3)
                block = add_half(block, way, decode(half_in.at[part, i, way]))
                encode(block, near_out.at[part, i, way])
                near_copy(part, i, way).start()
        return carry

    def item_z_copy(o):
        return copy(
            item_out.at[o - 1], item_z.at[o - 1], item_z_send.at[o - 1], item_z_recv.at[o - 1],
            device(turn(z, o, 8), y, x, c),
        )

    lax.fori_loop(0, 8, half_step, 0)
    item_first.wait_recv()
    item_half[...] = item_sums[pl.ds(c * 4, 4)].reshape(512, 128) + item_in[...].reshape(512, 128)

    def item_step_z(o, carry):
        zz = turn(z, o, 8)
        encode(item_half[pl.ds(pl.multiple_of(zz * 64, 64), 64)], item_out.at[o - 1])
        item_z_copy(o).start()
        return carry

    lax.fori_loop(1, 8, item_step_z, 0)
    lax.fori_loop(0, 8, near_step, 0)

    def plane_total(i):
        zz = turn(z, offset_of(i), 8)
        for part in (0, 1):
            for way in (0, 1):
                near_copy(part, i, way).wait_recv()
            value = plane_block(part, zz, 0)
            for way in (0, 1):
                value += decode(near_in.at[part, i, way])
            total[part, lax.rem(i, 2)] = value

    def z_where(way):
        return device(turn(z, 1 + 6 * way, 8), y, x, c)

    def far_copy(part, way):
        return copy(
            far_out.at[part, way], far_in.at[part, way], far_send.at[part, way], far_recv.at[part, way],
            z_where(way),
        )

    def column_copy(part, distance, way):
        return copy(
            column_out.at[part, distance - 1, way], column_in.at[part, distance - 1, way],
            column_send.at[part, distance - 1, way], column_recv.at[part, distance - 1, way],
            z_where(way),
        )

    def far_step():
        for part in (0, 1):
            for way in (0, 1):
                encode(total[part, 0, 128 * way:128 * way + 128], far_out.at[part, way])
                far_copy(part, way).start()

    def third_step(way):
        for part in (0, 1):
            far_copy(part, way).wait_recv()
            value = add_half(total[part, 1 - way], way, decode(far_in.at[part, way]))
            encode(value, column_out.at[part, 2, way])
            column_copy(part, 3, way).start()

    def column_step(i):
        way = 1 - lax.rem(i, 2)
        distance = 4 - (i + 1) // 2
        for part in (0, 1):
            column_copy(part, distance + 1, way).wait_recv()
            value = total[part, lax.rem(i, 2)] + decode(column_in.at[part, distance, way])
            encode(value, column_out.at[part, distance - 1, way])
            column_copy(part, distance, way).start()

    def both_step(i, carry):
        plane_total(i)
        column_step(i - 1)
        return carry

    plane_total(0)
    def item_gather(o, value):
        item_z_copy(o).wait_recv()
        return value + decode(item_z.at[o - 1])

    item_total = lax.fori_loop(
        1, 8, item_gather, item_half[pl.ds(pl.multiple_of(z * 64, 64), 64)]
    )
    item_pair_out[...] = item_total
    item_pair = copy(
        item_pair_out.at[pl.ds(pl.multiple_of((1 - ylo) * 32, 32), 32)], item_pair_in,
        item_send.at[1], item_recv.at[1], pair,
    )
    item_pair.start()
    plane_total(1)
    far_step()
    item_pair.wait_recv()
    encode(
        item_pair_out[pl.ds(pl.multiple_of(ylo * 32, 32), 32)] + item_pair_in[...],
        item_grads.at[c, z, ylo],
    )
    item_share = copy(
        item_grads.at[c, z, ylo], item_grads.at[c, z, ylo], item_send.at[2], item_recv.at[2], pair
    )
    item_share.start()
    plane_total(2)
    third_step(0)
    plane_total(3)
    third_step(1)
    item_share.wait_recv()

    def item_back(o):
        return copy(
            item_grads.at[c, z], item_grads.at[c, z], item_back_send.at[o - 1], item_back_recv.at[o - 1],
            device(turn(z, o, 8), y, x, c),
        )

    def item_back_start(o, carry):
        item_back(o).start()
        return carry

    lax.fori_loop(1, 8, item_back_start, 0)
    lax.fori_loop(4, 7, both_step, 0)
    column_step(6)
    plane_total(7)

    def item_back_wait(o, carry):
        item_back(o).wait_recv()
        return carry

    lax.fori_loop(1, 8, item_back_wait, 0)
    item_last = copy(item_grads.at[c], item_grads.at[c], item_send.at[3], item_recv.at[3], mate)
    item_last.start()

    for part in (0, 1):
        for way in (0, 1):
            column_copy(part, 1, way).wait_recv()
            total[part, 1] += decode(column_in.at[part, 0, way])

    def last_rows(part, k):
        if part == 0:
            other = turn(y, k, 4)
            place = lax.rem(other, 2) * 2 + other // 2
        else:
            place = turn(x, k, 4)
        return total[part, 1, pl.ds(pl.multiple_of(place * 64, 64), 64)]

    def last_copy(part, k):
        return copy(
            last_out.at[part, k - 1], last_in.at[part, k - 1],
            last_send.at[part, k - 1], last_recv.at[part, k - 1], plane_where(1 - part, k),
        )

    for k in (2, 1, 3):
        for part in (0, 1):
            encode(last_rows(part, k), last_out.at[part, k - 1])
            last_copy(part, k).start()

    item_last.wait_recv()

    def item_finish(n, carry):
        grad = decode(item_grads.at[n // 16, lax.rem(n // 2, 8), lax.rem(n, 2)])
        rows = pl.ds(pl.multiple_of(n * 32, 32), 32)
        now = own_items[rows].astype(jnp.float32)
        new_items[rows] = now - item_step * (grad + shrinkage * now)
        return carry

    lax.fori_loop(0, 32, item_finish, 0)

    halves = []
    for part in (0, 1):
        value = last_rows(part, 0)
        for k in (1, 2, 3):
            last_copy(part, k).wait_recv()
            value += decode(last_in.at[part, k - 1])
        halves.append(value)
    encode(jnp.concatenate(halves, axis=0), grads.at[q])

    def grad_copy(m):
        other = turn(q, m, 8)
        return copy(
            grads.at[q], grads.at[q], grad_send.at[m - 1], grad_recv.at[m - 1],
            device(z, (other // 4) * 2 + ylo, lax.rem(other, 4), c),
        )

    for m in range(1, 8):
        grad_copy(m).start()

    def plane_drain(i, carry):
        for part in (0, 1):
            for way in (0, 1):
                half_copy(part, i, way).wait_send()
                near_copy(part, i, way).wait_send()
        return carry

    def item_drain(o, carry):
        item_z_copy(o).wait_send()
        item_back(o).wait_send()
        return carry

    lax.fori_loop(0, 8, plane_drain, 0)
    lax.fori_loop(1, 8, item_drain, 0)
    for part in (0, 1):
        for way in (0, 1):
            far_copy(part, way).wait_send()
            for distance in (1, 2, 3):
                column_copy(part, distance, way).wait_send()
    for part in (0, 1):
        for k in (1, 2, 3):
            last_copy(part, k).wait_send()
    for early in (item_first, item_pair, item_share, item_last):
        early.wait_send()

    for m in range(1, 8):
        grad_copy(m).wait_recv()

    def user_finish(j, carry):
        grad = decode(grads.at[j])
        rows = pl.ds(pl.multiple_of(j * 128, 128), 128)
        now = own_users[rows].astype(jnp.float32)
        new_users[rows] = now - user_step * (grad + shrinkage * now)
        return carry

    lax.fori_loop(0, 8, user_finish, 0)
    for m in range(1, 8):
        grad_copy(m).wait_send()


def reduce(sums, item_sums, own_users, own_items):
    vmem = pl.BlockSpec(memory_space=pltpu.VMEM)
    dma = pltpu.SemaphoreType.DMA
    i16, f32 = jnp.int16, jnp.float32
    half = (2, 8, 2, 128 + SCALE_ROWS, 128)
    near = (2, 8, 2, 256 + SCALE_ROWS, 128)
    far = (2, 2, 128 + SCALE_ROWS, 128)
    column = (2, 3, 2, 256 + SCALE_ROWS, 128)
    last = (2, 3, 64 + SCALE_ROWS, 128)
    return pl.pallas_call(
        reduce_kernel,
        out_shape=(
            jax.ShapeDtypeStruct((1024, 128), f32),
            jax.ShapeDtypeStruct((1024, 128), f32),
        ),
        in_specs=[vmem, vmem, vmem, vmem],
        out_specs=(vmem, vmem),
        scratch_shapes=[
            pltpu.VMEM(half, i16), pltpu.VMEM(half, i16),
            pltpu.VMEM(near, i16), pltpu.VMEM(near, i16),
            pltpu.VMEM(far, i16), pltpu.VMEM(far, i16),
            pltpu.VMEM(column, i16), pltpu.VMEM(column, i16),
            pltpu.VMEM((2, 2, 256, 128), f32),
            pltpu.VMEM(last, i16), pltpu.VMEM(last, i16),
            pltpu.VMEM((8, 128 + SCALE_ROWS, 128), i16),
            pltpu.VMEM((4, 128, 128), f32), pltpu.VMEM((512, 128), f32),
            pltpu.VMEM((7, 64 + SCALE_ROWS, 128), i16), pltpu.VMEM((7, 64 + SCALE_ROWS, 128), i16),
            pltpu.VMEM((64, 128), f32), pltpu.VMEM((32, 128), f32),
            pltpu.VMEM((2, 8, 2, 32 + SCALE_ROWS, 128), i16),
            dma((2, 8, 2)), dma((2, 8, 2)), dma((2, 8, 2)), dma((2, 8, 2)),
            dma((2, 2)), dma((2, 2)), dma((2, 3, 2)), dma((2, 3, 2)),
            dma((2, 3)), dma((2, 3)), dma((7,)), dma((7,)),
            dma((4,)), dma((4,)), dma((7,)), dma((7,)), dma((7,)), dma((7,)),
        ],
        compiler_params=pltpu.CompilerParams(
            collective_id=1, has_side_effects=True, vmem_limit_bytes=16 * 2**20
        ),
    )(sums.reshape(8, 2, 2, 4, 128, 128), item_sums, own_users, own_items)


def body(user_factors, item_factors, block_user, block_item, live_blocks, ratings):
    slots = ratings.shape[2]
    scores = ratings.reshape(slots, 128, 128)
    lists = jnp.concatenate(
        [
            block_user.reshape(1, slots),
            block_item.reshape(1, slots),
            jnp.broadcast_to(live_blocks.reshape(1, 1), (1, slots)),
            jnp.zeros((5, slots), jnp.int32),
        ],
        axis=0,
    )
    users, all_scores, all_lists, no_users, no_items = gather(user_factors, scores, lists)
    core = lax.rem(lax.axis_index("user"), 2).astype(jnp.int32).reshape(1)
    user_sums, item_sums = local(
        core, all_lists, users.reshape(128, 128, 128), item_factors.reshape(8, 128, 128),
        all_scores.reshape(256, 128, 128), no_users, no_items,
    )
    return reduce(user_sums, item_sums, user_factors, item_factors)


def solution(mesh):
    return jax.shard_map(
        body,
        mesh=mesh,
        in_specs=(
            P("user", None),
            P("item", None),
            P("user", "item", None),
            P("user", "item", None),
            P("user", "item"),
            P("user", "item", None, None, None),
        ),
        out_specs=(P("user", None), P("item", None)),
        check_vma=False,
    )
```

```python
import functools

import jax
import jax.numpy as jnp
from jax import lax
from jax.experimental import pallas as pl
from jax.experimental.pallas import tpu as pltpu
from jax.sharding import PartitionSpec as P

MESH = pl.DeviceIdType.MESH


def here():
    p = lax.axis_index("user")
    q = lax.axis_index("item")
    return p // 4, lax.rem(p // 2, 2), q // 4, lax.rem(q, 4), lax.rem(p, 2)


def device(z, y, x, c):
    return (z * 4 + lax.rem(y, 2) * 2 + c, (y // 2) * 4 + x)


def neighbours():
    z, ylo, yhi, x, c = here()
    y = yhi * 2 + ylo
    up = lambda v, n: lax.rem(v + 1, n)
    down = lambda v, n: lax.rem(v + n - 1, n)
    return {
        "x": (device(z, y, up(x, 4), c), device(z, y, down(x, 4), c)),
        "y": (device(z, up(y, 4), x, c), device(z, down(y, 4), x, c)),
        "z": (device(up(z, 8), y, x, c), device(down(z, 8), y, x, c)),
        "pair": device(z, yhi * 2 + 1 - ylo, x, c),
        "mate": device(z, y, x, 1 - c),
    }


def meet(near):
    barrier = pltpu.get_barrier_semaphore()
    others = [*near["x"], *near["y"], *near["z"], near["mate"]]
    for other in others:
        pl.semaphore_signal(barrier, inc=1, device_id=other, device_id_type=MESH)
    pl.semaphore_wait(barrier, len(others))


class Sender:
    def __init__(self, send_sems, recv_sems):
        self.send_sems, self.recv_sems, self.used, self.copies = send_sems, recv_sems, 0, []

    def __call__(self, src, dst, where):
        copy = pltpu.make_async_remote_copy(
            src_ref=src,
            dst_ref=dst,
            send_sem=self.send_sems.at[self.used],
            recv_sem=self.recv_sems.at[self.used],
            device_id=where,
            device_id_type=MESH,
        )
        copy.start()
        self.used += 1
        self.copies.append(copy)
        return copy

    def drain(self):
        for copy in self.copies:
            copy.wait_send()


ROWS_A, ROWS_B, ROWS_C = 48, 48, 32
GATHER_COPIES = 160


def gather_kernel(split, own, ratings, lists, users, all_ratings, all_lists, no_users, no_items, local_sems, send_sems, recv_sems):
    z, ylo, yhi, x, c = here()
    y = yhi * 2 + ylo
    near = neighbours()
    keep = pltpu.make_async_copy(own, users.at[z, ylo], local_sems.at[0])
    keep.start()
    near_lists = pltpu.make_async_copy(lists, all_lists.at[c], local_sems.at[1])
    near_lists.start()
    near_ratings = pltpu.make_async_copy(ratings, all_ratings.at[c], local_sems.at[2])
    near_ratings.start()
    meet(near)
    send = Sender(send_sems, recv_sems)
    keep.wait()
    rows_a = pl.ds(0, split[0])
    rows_b = pl.ds(split[0], split[1])
    rows_c = pl.ds(split[0] + split[1], split[2])

    def zed(offset):
        return lax.rem(z + offset + 8, 8)

    def part_a(zz, low, xx, half=None):
        if half is None:
            return users.at[zz, low, :, xx, rows_a]
        return users.at[zz, low, half, xx, rows_a]

    def part_b(zz, yy, half=None):
        if half is None:
            return users.at[zz, lax.rem(yy, 2), yy // 2, :, rows_b]
        return users.at[zz, lax.rem(yy, 2), yy // 2, pl.ds(2 * half, 2), rows_b]

    def part_c(zz, low, half=None):
        if half is None:
            return users.at[zz, low, :, :, rows_c]
        return users.at[zz, low, half, :, rows_c]

    parts = {
        "A": lambda zz, half=None: part_a(zz, ylo, x, half),
        "B": lambda zz, half=None: part_b(zz, y, half),
        "C": lambda zz, half=None: part_c(zz, ylo, half),
        "D": lambda zz, half=None: part_c(zz, 1 - ylo, half),
    }
    along_z, pair, first, last = {}, {}, {}, []

    def z_send(name, step):
        for way in (0, 1):
            offset = -(step - 1) if way == 0 else step - 1
            block = parts[name](zed(offset), way if step == 4 else None)
            along_z[name, step, way] = send(block, block, near["z"][way])

    def z_wait(name, step):
        for way in (0, 1):
            along_z[name, step, way].wait_recv()

    def pair_send(offset):
        block = part_a(zed(offset), ylo, x)
        pair[offset] = send(block, block, near["pair"])

    late = (-3, 3, 4)

    def direct(block, where):
        last.append(send(block, block, where))

    def x_send(offset, low):
        if offset == 0 and low == 0 or offset == 4 and low == 1:
            return
        if offset in late:
            block = part_a(zed(offset), ylo if low == 0 else 1 - ylo, x)
            rows = (y, yhi * 2 + 1 - ylo) if offset == 4 else (y,)
            for k in (2, 1, 3):
                for row in rows:
                    direct(block, device(z, row, lax.rem(x + k, 4), c))
            return
        block = part_a(zed(offset), ylo if low == 0 else 1 - ylo, x)
        first["x", offset, low] = [send(block, block, near["x"][way]) for way in (0, 1)]

    def y_send(offset):
        if offset in late:
            block = part_b(zed(offset), y)
            for k in (2, 1, 3):
                direct(block, device(z, lax.rem(y + k, 4), x, c))
            return
        block = part_b(zed(offset), y)
        first["y", offset, 0] = [send(block, block, near["y"][way]) for way in (0, 1)]

    def forward(axis, offset, low):
        zz = zed(offset)
        if axis == "x" and offset == 0 and low == 0 or offset in late:
            return
        for way in (0, 1):
            first[axis, offset, low][way].wait_recv()
            if axis == "y" and offset == 0:
                continue
            back = 3 if way == 0 else 1
            if axis == "x":
                block = part_a(zz, ylo if low == 0 else 1 - ylo, lax.rem(x + back, 4), way)
            else:
                block = part_b(zz, lax.rem(y + back, 4), way)
            last.append(send(block, block, near[axis][way]))

    z_send("A", 1)
    z_send("B", 1)
    pair_c = send(part_c(z, ylo), part_c(z, ylo), near["pair"])
    pair_send(0)
    z_send("C", 1)
    x_send(0, 0)
    y_send(0)
    far = send(ratings, all_ratings.at[c], near["mate"])
    far_lists = send(lists, all_lists.at[c], near["mate"])
    no_items[...] = jnp.zeros_like(no_items)

    def clear(k, carry):
        no_users[k] = jnp.zeros(no_users.shape[1:], jnp.float32)
        return carry

    lax.fori_loop(0, no_users.shape[0], clear, 0)
    before = [0]
    for step in (1, 2, 3, 4):
        offsets = [-step, step] if step < 4 else [4]
        z_wait("A", step)
        if step < 4:
            z_send("A", step + 1)
        z_wait("B", step)
        if step < 4:
            z_send("B", step + 1)
        for offset in offsets:
            pair_send(offset)
            x_send(offset, 0)
            y_send(offset)
        if step == 1:
            pair_c.wait_recv()
            z_send("D", 1)
        z_wait("C", step)
        if step < 4:
            z_send("C", step + 1)
        for offset in before:
            pair[offset].wait_recv()
            x_send(offset, 1)
        for offset in before:
            forward("y", offset, 0)
            forward("x", offset, 0)
        if step > 1:
            z_wait("D", step - 1)
            z_send("D", step)
            for offset in earlier:
                forward("x", offset, 1)
        earlier, before = before, offsets
    for offset in before:
        pair[offset].wait_recv()
        x_send(offset, 1)
    for offset in before:
        forward("y", offset, 0)
        forward("x", offset, 0)
    for offset in earlier + before:
        forward("x", offset, 1)
    z_wait("D", 4)
    for copy in last:
        copy.wait_recv()
    near_lists.wait()
    near_ratings.wait()
    far.wait_recv()
    far_lists.wait_recv()
    send.drain()


def gather(user_factors, ratings, lists, vmem=True):
    space = pltpu.VMEM if vmem else pl.ANY
    return pl.pallas_call(
        functools.partial(gather_kernel, (ROWS_A, ROWS_B, ROWS_C)),
        out_shape=(
            jax.ShapeDtypeStruct((8, 2, 2, 4, 128, 128), jnp.bfloat16),
            jax.ShapeDtypeStruct((2, *ratings.shape), jnp.int32),
            jax.ShapeDtypeStruct((2, *lists.shape), jnp.int32),
            jax.ShapeDtypeStruct((128, 128, 128), jnp.float32),
            jax.ShapeDtypeStruct((8, 128, 128), jnp.float32),
        ),
        in_specs=[
            pl.BlockSpec(memory_space=pltpu.HBM),
            pl.BlockSpec(memory_space=pltpu.HBM),
            pl.BlockSpec(memory_space=pltpu.VMEM),
        ],
        out_specs=(
            pl.BlockSpec(memory_space=space),
            pl.BlockSpec(memory_space=space),
            pl.BlockSpec(memory_space=pltpu.VMEM),
            pl.BlockSpec(memory_space=pltpu.VMEM),
            pl.BlockSpec(memory_space=pltpu.VMEM),
        ),
        scratch_shapes=[
            pltpu.SemaphoreType.DMA((3,)),
            pltpu.SemaphoreType.DMA((GATHER_COPIES,)),
            pltpu.SemaphoreType.DMA((GATHER_COPIES,)),
        ],
        compiler_params=pltpu.CompilerParams(
            collective_id=0, has_side_effects=True, vmem_limit_bytes=8 * 2**20
        ),
    )(
        pltpu.with_memory_space_constraint(user_factors.reshape(2, 4, 128, 128), pltpu.HBM),
        pltpu.with_memory_space_constraint(ratings, pltpu.HBM),
        lists,
    )


GROUP = 16


def local_kernel(core, lists, users, items, ratings, no_users, no_items, user_sum, item_sum, order):
    mine = core[0]

    def scan(table):
        def visit(slot, count):
            block = lists[table, 0, slot]
            order[count] = ((table * 128 + slot) * 256 + block) * 8 + lists[table, 1, slot]
            keep = lax.rem(block // 8, 2) == mine
            return count + keep.astype(jnp.int32)
        return visit

    count = lax.fori_loop(0, lists[0, 2, 0], scan(0), jnp.int32(0))
    count = lax.fori_loop(0, lists[1, 2, 0], scan(1), count)
    for k in range(GROUP):
        order[count + k] = 0

    def step(g, carry):
        first = g * GROUP
        records = []
        for k in range(GROUP):
            n = first + k
            entry = order[n]
            item = lax.rem(entry, 8)
            block = lax.rem(entry // 8, 256)
            tile = (block // 16) * 8 + lax.rem(block, 8)
            user_tile = users[tile]
            item_tile = items[item]
            predicted = lax.dot_general(
                user_tile, item_tile, (((1,), (1,)), ((), ())), preferred_element_type=jnp.float32
            )
            scores = ratings[entry // 2048]
            floor = jnp.where(n < count, 0, 1 << 20)
            errors = jnp.where(
                scores > floor, predicted - (scores.astype(jnp.float32) - 3.0), 0.0
            ).astype(jnp.bfloat16)
            records.append((tile, item, user_tile, item_tile, errors))
        terms = []
        for tile, item, user_tile, item_tile, errors in records:
            user_term = jnp.dot(errors, item_tile, preferred_element_type=jnp.float32)
            item_term = lax.dot_general(
                errors, user_tile, (((0,), (0,)), ((), ())), preferred_element_type=jnp.float32
            )
            terms.append((tile, item, user_term, item_term))
        for tile, item, user_term, item_term in terms:
            user_sum[tile] += user_term
            item_sum[item] += item_term
        return carry

    lax.fori_loop(0, (count + GROUP - 1) // GROUP, step, 0)


def local(core, lists, users, items, ratings, no_users, no_items):
    smem = pl.BlockSpec(memory_space=pltpu.SMEM)
    vmem = pl.BlockSpec(memory_space=pltpu.VMEM)
    return pl.pallas_call(
        local_kernel,
        out_shape=(
            jax.ShapeDtypeStruct((128, 128, 128), jnp.float32),
            jax.ShapeDtypeStruct((8, 128, 128), jnp.float32),
        ),
        in_specs=[smem, smem, vmem, vmem, vmem, vmem, vmem],
        out_specs=(vmem, vmem),
        input_output_aliases={5: 0, 6: 1},
        scratch_shapes=[pltpu.SMEM((256 + GROUP,), jnp.int32)],
        compiler_params=pltpu.CompilerParams(vmem_limit_bytes=8 * 2**20),
    )(core, lists, users, items, ratings, no_users, no_items)


user_step = 0.1
item_step = 0.04
shrinkage = 0.1
EDGE_ROWS, MIDDLE_ROWS = 56, 16
CHUNK = 4 * EDGE_ROWS


def coded_rows(rows):
    return rows + (16 if rows % 16 == 0 else 8)


def encode(value, buffer):
    rows = value.shape[0]
    folded = value.reshape(rows // 8, 8, 128)
    peak = jnp.maximum(jnp.max(jnp.abs(folded), axis=0), 1e-30)
    power = jnp.ceil(jnp.log2(peak))
    whole = jnp.round(folded * jnp.exp2(14.0 - power)).reshape(rows, 128)
    tail = [power] * ((coded_rows(rows) - rows) // 8)
    buffer[...] = jnp.concatenate([whole, *tail], axis=0).astype(jnp.int32).astype(jnp.int16)


def decode(buffer, rows):
    every = coded_rows(rows)
    power = buffer[every - 16:every].astype(jnp.float32)[8:16]
    folded = buffer[...].astype(jnp.float32)[0:rows].reshape(rows // 8, 8, 128)
    return (folded * jnp.exp2(power - 14.0)).reshape(rows, 128)


def reduce_kernel(
    sums, item_sums, own_users, own_items, new_users, new_items,
    half_out, half_in, near_out, near_in, far_out, far_in, column_out, column_in, total,
    last_out, last_in, grads,
    mid_far_out, mid_far_in, mid_out, mid_in, mid_total, mid_y_out, mid_y_in, mid_row, mid_x_out, mid_x_in, mid_grads,
    item_in, item_half, item_pair_out, item_pair_in, item_row, item_out, item_z, item_grads,
    half_send, half_recv, near_send, near_recv, far_send, far_recv, column_send, column_recv,
    last_send, last_recv, grad_send, grad_recv,
    mid_far_send, mid_far_recv, mid_send, mid_recv, mid_y_send, mid_y_recv, mid_x_send, mid_x_recv,
    mid_grad_send, mid_grad_recv,
    item_send, item_recv, item_z_send, item_z_recv, item_back_send, item_back_recv,
):
    z, ylo, yhi, x, c = here()
    y = yhi * 2 + ylo
    q = yhi * 4 + x

    def turn(v, k, n):
        return lax.rem(v + k, n)

    def copy(src, dst, send_sem, recv_sem, where):
        return pltpu.make_async_remote_copy(
            src_ref=src, dst_ref=dst, send_sem=send_sem, recv_sem=recv_sem,
            device_id=where, device_id_type=MESH,
        )

    def offset_of(i):
        return 4 + (1 - 2 * lax.rem(i, 2)) * ((i + 1) // 2)

    barrier = pltpu.get_barrier_semaphore()
    others = [device(z, y, turn(x, k, 4), c) for k in (1, 3)]
    others += [device(z, turn(y, k, 4), x, c) for k in (1, 3)]
    others += [device(turn(z, k, 8), y, x, c) for k in (1, 7)]
    others += [device(z, y, x, 1 - c)]
    for other in others:
        pl.semaphore_signal(barrier, inc=1, device_id=other, device_id_type=MESH)
    pl.semaphore_wait(barrier, len(others))

    mate = device(z, y, x, 1 - c)
    pair = device(z, yhi * 2 + 1 - ylo, x, c)
    item_first = copy(item_sums.at[pl.ds((1 - c) * 4, 4)], item_in, item_send.at[0], item_recv.at[0], mate)
    item_first.start()

    def plane_where(part, k):
        return device(z, y, turn(x, k, 4), c) if part == 0 else device(z, turn(y, k, 4), x, c)

    def plane_block(part, zz, k):
        if part == 0:
            return sums[zz, :, :, turn(x, k, 4), 0:EDGE_ROWS].reshape(CHUNK, 128)
        other = turn(y, k, 4)
        return sums[zz, lax.rem(other, 2), other // 2, :, EDGE_ROWS:2 * EDGE_ROWS].reshape(CHUNK, 128)

    def toward(part, way):
        return plane_where(part, 1 if way == 0 else 3)

    def half_copy(part, i, way):
        return copy(
            half_out.at[part, i, way], half_in.at[part, i, way],
            half_send.at[part, i, way], half_recv.at[part, i, way], toward(part, way),
        )

    def near_copy(part, i, way):
        return copy(
            near_out.at[part, i, way], near_in.at[part, i, way],
            near_send.at[part, i, way], near_recv.at[part, i, way], toward(part, way),
        )

    def add_half(value, way, extra):
        split = value.shape[0] // 2
        if way == 0:
            return jnp.concatenate([value[0:split] + extra, value[split:]], axis=0)
        return jnp.concatenate([value[0:split], value[split:] + extra], axis=0)

    def half_step(i, carry):
        zz = turn(z, offset_of(i), 8)
        for way in (0, 1):
            for part in (0, 1):
                block = plane_block(part, zz, 2)[CHUNK // 2 * way:CHUNK // 2 * (way + 1)]
                encode(block, half_out.at[part, i, way])
                half_copy(part, i, way).start()
        return carry

    def near_step(i, carry):
        zz = turn(z, offset_of(i), 8)
        for way in (0, 1):
            for part in (0, 1):
                half_copy(part, i, way).wait_recv()
                block = plane_block(part, zz, 1 if way == 0 else 3)
                block = add_half(block, way, decode(half_in.at[part, i, way], CHUNK // 2))
                encode(block, near_out.at[part, i, way])
                near_copy(part, i, way).start()
        return carry

    def plane_total(i):
        zz = turn(z, offset_of(i), 8)
        for part in (0, 1):
            for way in (0, 1):
                near_copy(part, i, way).wait_recv()
            value = plane_block(part, zz, 0)
            for way in (0, 1):
                value += decode(near_in.at[part, i, way], CHUNK)
            total[part, lax.rem(i, 2)] = value

    def z_where(way):
        return device(turn(z, 1 + 6 * way, 8), y, x, c)

    def far_copy(part, way):
        return copy(
            far_out.at[part, way], far_in.at[part, way], far_send.at[part, way], far_recv.at[part, way],
            z_where(way),
        )

    def column_copy(part, distance, way):
        return copy(
            column_out.at[part, distance - 1, way], column_in.at[part, distance - 1, way],
            column_send.at[part, distance - 1, way], column_recv.at[part, distance - 1, way],
            z_where(way),
        )

    def far_step():
        for part in (0, 1):
            for way in (0, 1):
                encode(total[part, 0, CHUNK // 2 * way:CHUNK // 2 * (way + 1)], far_out.at[part, way])
                far_copy(part, way).start()

    def third_step(way):
        for part in (0, 1):
            far_copy(part, way).wait_recv()
            value = add_half(total[part, 1 - way], way, decode(far_in.at[part, way], CHUNK // 2))
            encode(value, column_out.at[part, 2, way])
            column_copy(part, 3, way).start()

    def column_step(i):
        way = 1 - lax.rem(i, 2)
        distance = 4 - (i + 1) // 2
        for part in (0, 1):
            column_copy(part, distance + 1, way).wait_recv()
            value = total[part, lax.rem(i, 2)] + decode(column_in.at[part, distance, way], CHUNK)
            encode(value, column_out.at[part, distance - 1, way])
            column_copy(part, distance, way).start()

    def both_step(i, carry):
        plane_total(i)
        column_step(i - 1)
        return carry

    def mid_block(zz):
        return sums[zz, :, :, :, 2 * EDGE_ROWS:128].reshape(16 * MIDDLE_ROWS, 128)

    def mid_far_copy(way):
        return copy(
            mid_far_out.at[way], mid_far_in.at[way], mid_far_send.at[way], mid_far_recv.at[way], z_where(way)
        )

    def mid_copy(distance, way):
        return copy(
            mid_out.at[distance - 1, way], mid_in.at[distance - 1, way],
            mid_send.at[distance - 1, way], mid_recv.at[distance - 1, way], z_where(way),
        )

    def mid_far():
        for way in (0, 1):
            block = mid_block(turn(z, 4, 8))[8 * MIDDLE_ROWS * way:8 * MIDDLE_ROWS * (way + 1)]
            encode(block, mid_far_out.at[way])
            mid_far_copy(way).start()

    def mid_step(distance):
        for way in (0, 1):
            block = mid_block(turn(z, distance if way == 0 else 8 - distance, 8))
            if distance == 3:
                mid_far_copy(way).wait_recv()
                block = add_half(block, way, decode(mid_far_in.at[way], 8 * MIDDLE_ROWS))
            else:
                mid_copy(distance + 1, way).wait_recv()
                block += decode(mid_in.at[distance, way], 16 * MIDDLE_ROWS)
            encode(block, mid_out.at[distance - 1, way])
            mid_copy(distance, way).start()

    def mid_y_copy(k):
        return copy(
            mid_y_out.at[k - 1], mid_y_in.at[k - 1], mid_y_send.at[k - 1], mid_y_recv.at[k - 1],
            plane_where(1, k),
        )

    def mid_x_copy(k):
        return copy(
            mid_x_out.at[k - 1], mid_x_in.at[k - 1], mid_x_send.at[k - 1], mid_x_recv.at[k - 1],
            plane_where(0, k),
        )

    def mid_y_rows(k):
        other = turn(y, k, 4)
        place = lax.rem(other, 2) * 2 + other // 2
        size = 4 * MIDDLE_ROWS
        return mid_total[pl.ds(pl.multiple_of(place * size, size), size)]

    def mid_x_rows(k):
        return mid_row[pl.ds(pl.multiple_of(turn(x, k, 4) * MIDDLE_ROWS, MIDDLE_ROWS), MIDDLE_ROWS)]

    def mid_to_y():
        value = mid_block(z)
        for way in (0, 1):
            mid_copy(1, way).wait_recv()
            value += decode(mid_in.at[0, way], 16 * MIDDLE_ROWS)
        mid_total[...] = value
        for k in (2, 1, 3):
            encode(mid_y_rows(k), mid_y_out.at[k - 1])
            mid_y_copy(k).start()

    def mid_to_x():
        value = mid_y_rows(0)
        for k in (1, 2, 3):
            mid_y_copy(k).wait_recv()
            value += decode(mid_y_in.at[k - 1], 4 * MIDDLE_ROWS)
        mid_row[...] = value
        for k in (2, 1, 3):
            encode(mid_x_rows(k), mid_x_out.at[k - 1])
            mid_x_copy(k).start()

    def q_where(m):
        other = turn(q, m, 8)
        return device(z, (other // 4) * 2 + ylo, lax.rem(other, 4), c)

    def mid_grad_copy(m):
        return copy(
            mid_grads.at[q], mid_grads.at[q], mid_grad_send.at[m - 1], mid_grad_recv.at[m - 1], q_where(m)
        )

    def mid_finish():
        value = mid_x_rows(0)
        for k in (1, 2, 3):
            mid_x_copy(k).wait_recv()
            value += decode(mid_x_in.at[k - 1], MIDDLE_ROWS)
        encode(value, mid_grads.at[q])
        for m in range(1, 8):
            mid_grad_copy(m).start()

    item_pair = copy(item_pair_out, item_pair_in, item_send.at[1], item_recv.at[1], pair)

    def item_to_pair():
        item_first.wait_recv()
        item_half[...] = item_sums[pl.ds(c * 4, 4)].reshape(512, 128) + item_in[...].reshape(512, 128)
        encode(item_half[pl.ds(pl.multiple_of((1 - ylo) * 256, 256), 256)], item_pair_out)
        item_pair.start()

    def item_z_copy(o):
        return copy(
            item_out.at[o - 1], item_z.at[o - 1], item_z_send.at[o - 1], item_z_recv.at[o - 1],
            device(turn(z, o, 8), y, x, c),
        )

    def item_rows(zz):
        return item_row[pl.ds(pl.multiple_of(zz * 32, 32), 32)]

    def item_to_z():
        item_pair.wait_recv()
        own = item_half[pl.ds(pl.multiple_of(ylo * 256, 256), 256)]
        item_row[...] = own + decode(item_pair_in, 256)

        def each(o, carry):
            encode(item_rows(turn(z, o, 8)), item_out.at[o - 1])
            item_z_copy(o).start()
            return carry

        lax.fori_loop(1, 8, each, 0)

    def item_back(o):
        return copy(
            item_grads.at[c, ylo, z], item_grads.at[c, ylo, z], item_back_send.at[o - 1], item_back_recv.at[o - 1],
            device(turn(z, o, 8), y, x, c),
        )

    def item_total():
        def each(o, value):
            item_z_copy(o).wait_recv()
            return value + decode(item_z.at[o - 1], 32)

        encode(lax.fori_loop(1, 8, each, item_rows(z)), item_grads.at[c, ylo, z])

        def start(o, carry):
            item_back(o).start()
            return carry

        lax.fori_loop(1, 8, start, 0)

    item_share = copy(
        item_grads.at[c, ylo], item_grads.at[c, ylo], item_send.at[2], item_recv.at[2], pair
    )
    item_last = copy(item_grads.at[c], item_grads.at[c], item_send.at[3], item_recv.at[3], mate)

    def item_to_share():
        def each(o, carry):
            item_back(o).wait_recv()
            return carry

        lax.fori_loop(1, 8, each, 0)
        item_share.start()

    def last_rows(part, k):
        if part == 0:
            other = turn(y, k, 4)
            place = lax.rem(other, 2) * 2 + other // 2
        else:
            place = turn(x, k, 4)
        return total[part, 1, pl.ds(pl.multiple_of(place * EDGE_ROWS, 8), EDGE_ROWS)]

    def last_copy(part, k):
        return copy(
            last_out.at[part, k - 1], last_in.at[part, k - 1],
            last_send.at[part, k - 1], last_recv.at[part, k - 1], plane_where(1 - part, k),
        )

    def grad_copy(m):
        return copy(grads.at[q], grads.at[q], grad_send.at[m - 1], grad_recv.at[m - 1], q_where(m))

    mid_far()
    lax.fori_loop(0, 8, half_step, 0)
    item_to_pair()
    mid_step(3)
    lax.fori_loop(0, 4, near_step, 0)
    mid_step(2)
    lax.fori_loop(4, 8, near_step, 0)
    plane_total(0)
    mid_step(1)
    plane_total(1)
    far_step()
    plane_total(2)
    third_step(0)
    mid_to_y()
    plane_total(3)
    third_step(1)
    item_to_z()
    lax.fori_loop(4, 6, both_step, 0)
    mid_to_x()
    both_step(6, 0)
    column_step(6)
    item_total()
    mid_finish()
    plane_total(7)
    for part in (0, 1):
        for way in (0, 1):
            column_copy(part, 1, way).wait_recv()
            total[part, 1] += decode(column_in.at[part, 0, way], CHUNK)
    for k in (2, 1, 3):
        for part in (0, 1):
            encode(last_rows(part, k), last_out.at[part, k - 1])
            last_copy(part, k).start()
    item_to_share()
    halves = []
    for part in (0, 1):
        value = last_rows(part, 0)
        for k in (1, 2, 3):
            last_copy(part, k).wait_recv()
            value += decode(last_in.at[part, k - 1], EDGE_ROWS)
        halves.append(value)
    encode(jnp.concatenate(halves, axis=0), grads.at[q])
    for m in range(1, 8):
        grad_copy(m).start()
    item_share.wait_recv()
    item_last.start()

    def plane_drain(i, carry):
        for part in (0, 1):
            for way in (0, 1):
                half_copy(part, i, way).wait_send()
                near_copy(part, i, way).wait_send()
        return carry

    def peer_drain(o, carry):
        item_z_copy(o).wait_send()
        item_back(o).wait_send()
        mid_grad_copy(o).wait_send()
        return carry

    lax.fori_loop(0, 8, plane_drain, 0)
    lax.fori_loop(1, 8, peer_drain, 0)
    for way in (0, 1):
        mid_far_copy(way).wait_send()
        for part in (0, 1):
            far_copy(part, way).wait_send()
        for distance in (1, 2, 3):
            mid_copy(distance, way).wait_send()
            for part in (0, 1):
                column_copy(part, distance, way).wait_send()
    for k in (1, 2, 3):
        mid_y_copy(k).wait_send()
        mid_x_copy(k).wait_send()
        for part in (0, 1):
            last_copy(part, k).wait_send()
    item_last.wait_recv()

    def item_finish(n, carry):
        grad = decode(item_grads.at[n // 16, lax.rem(n // 8, 2), lax.rem(n, 8)], 32)
        rows = pl.ds(pl.multiple_of(n * 32, 32), 32)
        now = own_items[rows].astype(jnp.float32)
        new_items[rows] = now - item_step * (grad + shrinkage * now)
        return carry

    lax.fori_loop(0, 32, item_finish, 0)
    for m in range(1, 8):
        mid_grad_copy(m).wait_recv()
    for m in range(1, 8):
        grad_copy(m).wait_recv()

    def user_finish(j, carry):
        grad = jnp.concatenate(
            [decode(grads.at[j], 2 * EDGE_ROWS), decode(mid_grads.at[j], MIDDLE_ROWS)], axis=0
        )
        rows = pl.ds(pl.multiple_of(j * 128, 128), 128)
        now = own_users[rows].astype(jnp.float32)
        new_users[rows] = now - user_step * (grad + shrinkage * now)
        return carry

    lax.fori_loop(0, 8, user_finish, 0)
    for m in range(1, 8):
        grad_copy(m).wait_send()
    for early in (item_first, item_pair, item_share, item_last):
        early.wait_send()


def reduce(sums, item_sums, own_users, own_items):
    vmem = pl.BlockSpec(memory_space=pltpu.VMEM)
    dma = pltpu.SemaphoreType.DMA
    i16, f32 = jnp.int16, jnp.float32
    half = (2, 8, 2, coded_rows(CHUNK // 2), 128)
    near = (2, 8, 2, coded_rows(CHUNK), 128)
    far = (2, 2, coded_rows(CHUNK // 2), 128)
    column = (2, 3, 2, coded_rows(CHUNK), 128)
    last = (2, 3, coded_rows(EDGE_ROWS), 128)
    mid_far = (2, coded_rows(8 * MIDDLE_ROWS), 128)
    mid = (3, 2, coded_rows(16 * MIDDLE_ROWS), 128)
    mid_y = (3, coded_rows(4 * MIDDLE_ROWS), 128)
    mid_x = (3, coded_rows(MIDDLE_ROWS), 128)
    item_z = (7, coded_rows(32), 128)
    item_pair = (coded_rows(256), 128)
    both = lambda shape: [pltpu.VMEM(shape, i16)] * 2
    sems = lambda *shape: [dma(shape)] * 2
    return pl.pallas_call(
        reduce_kernel,
        out_shape=(
            jax.ShapeDtypeStruct((1024, 128), f32),
            jax.ShapeDtypeStruct((1024, 128), f32),
        ),
        in_specs=[vmem, vmem, vmem, vmem],
        out_specs=(vmem, vmem),
        scratch_shapes=[
            *both(half), *both(near), *both(far), *both(column),
            pltpu.VMEM((2, 2, CHUNK, 128), f32),
            *both(last),
            pltpu.VMEM((8, coded_rows(2 * EDGE_ROWS), 128), i16),
            *both(mid_far), *both(mid),
            pltpu.VMEM((16 * MIDDLE_ROWS, 128), f32),
            *both(mid_y),
            pltpu.VMEM((4 * MIDDLE_ROWS, 128), f32),
            *both(mid_x),
            pltpu.VMEM((8, coded_rows(MIDDLE_ROWS), 128), i16),
            pltpu.VMEM((4, 128, 128), f32), pltpu.VMEM((512, 128), f32),
            *both(item_pair),
            pltpu.VMEM((256, 128), f32),
            *both(item_z),
            pltpu.VMEM((2, 2, 8, coded_rows(32), 128), i16),
            *sems(2, 8, 2), *sems(2, 8, 2), *sems(2, 2), *sems(2, 3, 2),
            *sems(2, 3), *sems(7),
            *sems(2), *sems(3, 2), *sems(3), *sems(3), *sems(7),
            *sems(4), *sems(7), *sems(7),
        ],
        compiler_params=pltpu.CompilerParams(
            collective_id=1, has_side_effects=True, vmem_limit_bytes=16 * 2**20
        ),
    )(sums.reshape(8, 2, 2, 4, 128, 128), item_sums, own_users, own_items)


def body(user_factors, item_factors, block_user, block_item, live_blocks, ratings):
    slots = ratings.shape[2]
    scores = ratings.reshape(slots, 128, 128)
    lists = jnp.concatenate(
        [
            block_user.reshape(1, slots),
            block_item.reshape(1, slots),
            jnp.broadcast_to(live_blocks.reshape(1, 1), (1, slots)),
            jnp.zeros((5, slots), jnp.int32),
        ],
        axis=0,
    )
    users, all_scores, all_lists, no_users, no_items = gather(user_factors, scores, lists)
    core = lax.rem(lax.axis_index("user"), 2).astype(jnp.int32).reshape(1)
    user_sums, item_sums = local(
        core, all_lists, users.reshape(128, 128, 128), item_factors.reshape(8, 128, 128),
        all_scores.reshape(256, 128, 128), no_users, no_items,
    )
    return reduce(user_sums, item_sums, user_factors, item_factors)


def solution(mesh):
    return jax.shard_map(
        body,
        mesh=mesh,
        in_specs=(
            P("user", None),
            P("item", None),
            P("user", "item", None),
            P("user", "item", None),
            P("user", "item"),
            P("user", "item", None, None, None),
        ),
        out_specs=(P("user", None), P("item", None)),
        check_vma=False,
    )
```

```python
import functools

import jax
import jax.numpy as jnp
from jax import lax
from jax.experimental import pallas as pl
from jax.experimental.pallas import tpu as pltpu
from jax.sharding import PartitionSpec as P

MESH = pl.DeviceIdType.MESH


def here():
    p = lax.axis_index("user")
    q = lax.axis_index("item")
    return p // 4, lax.rem(p // 2, 2), q // 4, lax.rem(q, 4), lax.rem(p, 2)


def device(z, y, x, c):
    return (z * 4 + lax.rem(y, 2) * 2 + c, (y // 2) * 4 + x)


def neighbours():
    z, ylo, yhi, x, c = here()
    y = yhi * 2 + ylo
    up = lambda v, n: lax.rem(v + 1, n)
    down = lambda v, n: lax.rem(v + n - 1, n)
    return {
        "x": (device(z, y, up(x, 4), c), device(z, y, down(x, 4), c)),
        "y": (device(z, up(y, 4), x, c), device(z, down(y, 4), x, c)),
        "z": (device(up(z, 8), y, x, c), device(down(z, 8), y, x, c)),
        "pair": device(z, yhi * 2 + 1 - ylo, x, c),
        "mate": device(z, y, x, 1 - c),
    }


def meet(near):
    barrier = pltpu.get_barrier_semaphore()
    others = [*near["x"], *near["y"], *near["z"], near["mate"]]
    for other in others:
        pl.semaphore_signal(barrier, inc=1, device_id=other, device_id_type=MESH)
    pl.semaphore_wait(barrier, len(others))


class Sender:
    def __init__(self, send_sems, recv_sems):
        self.send_sems, self.recv_sems, self.used, self.copies = send_sems, recv_sems, 0, []

    def __call__(self, src, dst, where):
        copy = pltpu.make_async_remote_copy(
            src_ref=src,
            dst_ref=dst,
            send_sem=self.send_sems.at[self.used],
            recv_sem=self.recv_sems.at[self.used],
            device_id=where,
            device_id_type=MESH,
        )
        copy.start()
        self.used += 1
        self.copies.append(copy)
        return copy

    def drain(self):
        for copy in self.copies:
            copy.wait_send()


ROWS_A, ROWS_B, ROWS_C = 48, 48, 32
GATHER_COPIES = 160


def gather_kernel(split, own, ratings, lists, users, all_ratings, all_lists, no_users, no_items, local_sems, send_sems, recv_sems):
    z, ylo, yhi, x, c = here()
    y = yhi * 2 + ylo
    near = neighbours()
    keep = pltpu.make_async_copy(own, users.at[z, ylo], local_sems.at[0])
    keep.start()
    near_lists = pltpu.make_async_copy(lists, all_lists.at[c], local_sems.at[1])
    near_lists.start()
    near_ratings = pltpu.make_async_copy(ratings, all_ratings.at[c], local_sems.at[2])
    near_ratings.start()
    meet(near)
    send = Sender(send_sems, recv_sems)
    keep.wait()
    rows_a = pl.ds(0, split[0])
    rows_b = pl.ds(split[0], split[1])
    rows_c = pl.ds(split[0] + split[1], split[2])

    def zed(offset):
        return lax.rem(z + offset + 8, 8)

    def part_a(zz, low, xx, half=None):
        if half is None:
            return users.at[zz, low, :, xx, rows_a]
        return users.at[zz, low, half, xx, rows_a]

    def part_b(zz, yy, half=None):
        if half is None:
            return users.at[zz, lax.rem(yy, 2), yy // 2, :, rows_b]
        return users.at[zz, lax.rem(yy, 2), yy // 2, pl.ds(2 * half, 2), rows_b]

    def part_c(zz, low, half=None):
        if half is None:
            return users.at[zz, low, :, :, rows_c]
        return users.at[zz, low, half, :, rows_c]

    parts = {
        "A": lambda zz, half=None: part_a(zz, ylo, x, half),
        "B": lambda zz, half=None: part_b(zz, y, half),
        "C": lambda zz, half=None: part_c(zz, ylo, half),
        "D": lambda zz, half=None: part_c(zz, 1 - ylo, half),
    }
    along_z, pair, first, last = {}, {}, {}, []

    def z_send(name, step):
        for way in (0, 1):
            offset = -(step - 1) if way == 0 else step - 1
            block = parts[name](zed(offset), way if step == 4 else None)
            along_z[name, step, way] = send(block, block, near["z"][way])

    def z_wait(name, step):
        for way in (0, 1):
            along_z[name, step, way].wait_recv()

    def pair_send(offset):
        block = part_a(zed(offset), ylo, x)
        pair[offset] = send(block, block, near["pair"])

    late = (-3, 3, 4)

    def direct(block, where):
        last.append(send(block, block, where))

    def x_send(offset, low):
        if offset == 0 and low == 0 or offset == 4 and low == 1:
            return
        if offset in late:
            block = part_a(zed(offset), ylo if low == 0 else 1 - ylo, x)
            rows = (y, yhi * 2 + 1 - ylo) if offset == 4 else (y,)
            for k in (2, 1, 3):
                for row in rows:
                    direct(block, device(z, row, lax.rem(x + k, 4), c))
            return
        block = part_a(zed(offset), ylo if low == 0 else 1 - ylo, x)
        first["x", offset, low] = [send(block, block, near["x"][way]) for way in (0, 1)]

    def y_send(offset):
        if offset in late:
            block = part_b(zed(offset), y)
            for k in (2, 1, 3):
                direct(block, device(z, lax.rem(y + k, 4), x, c))
            return
        block = part_b(zed(offset), y)
        first["y", offset, 0] = [send(block, block, near["y"][way]) for way in (0, 1)]

    def forward(axis, offset, low):
        zz = zed(offset)
        if axis == "x" and offset == 0 and low == 0 or offset in late:
            return
        for way in (0, 1):
            first[axis, offset, low][way].wait_recv()
            if axis == "y" and offset == 0:
                continue
            back = 3 if way == 0 else 1
            if axis == "x":
                block = part_a(zz, ylo if low == 0 else 1 - ylo, lax.rem(x + back, 4), way)
            else:
                block = part_b(zz, lax.rem(y + back, 4), way)
            last.append(send(block, block, near[axis][way]))

    z_send("A", 1)
    z_send("B", 1)
    pair_c = send(part_c(z, ylo), part_c(z, ylo), near["pair"])
    pair_send(0)
    z_send("C", 1)
    x_send(0, 0)
    y_send(0)
    far = send(ratings, all_ratings.at[c], near["mate"])
    far_lists = send(lists, all_lists.at[c], near["mate"])
    no_items[...] = jnp.zeros_like(no_items)

    def clear(k, carry):
        no_users[k] = jnp.zeros(no_users.shape[1:], jnp.float32)
        return carry

    lax.fori_loop(0, no_users.shape[0], clear, 0)
    before = [0]
    for step in (1, 2, 3, 4):
        offsets = [-step, step] if step < 4 else [4]
        z_wait("A", step)
        if step < 4:
            z_send("A", step + 1)
        z_wait("B", step)
        if step < 4:
            z_send("B", step + 1)
        for offset in offsets:
            pair_send(offset)
            x_send(offset, 0)
            y_send(offset)
        if step == 1:
            pair_c.wait_recv()
            z_send("D", 1)
        z_wait("C", step)
        if step < 4:
            z_send("C", step + 1)
        for offset in before:
            pair[offset].wait_recv()
            x_send(offset, 1)
        for offset in before:
            forward("y", offset, 0)
            forward("x", offset, 0)
        if step > 1:
            z_wait("D", step - 1)
            z_send("D", step)
            for offset in earlier:
                forward("x", offset, 1)
        earlier, before = before, offsets
    for offset in before:
        pair[offset].wait_recv()
        x_send(offset, 1)
    for offset in before:
        forward("y", offset, 0)
        forward("x", offset, 0)
    for offset in earlier + before:
        forward("x", offset, 1)
    z_wait("D", 4)
    for copy in last:
        copy.wait_recv()
    near_lists.wait()
    near_ratings.wait()
    far.wait_recv()
    far_lists.wait_recv()
    send.drain()


def gather(user_factors, ratings, lists, vmem=True):
    space = pltpu.VMEM if vmem else pl.ANY
    return pl.pallas_call(
        functools.partial(gather_kernel, (ROWS_A, ROWS_B, ROWS_C)),
        out_shape=(
            jax.ShapeDtypeStruct((8, 2, 2, 4, 128, 128), jnp.bfloat16),
            jax.ShapeDtypeStruct((2, *ratings.shape), jnp.int32),
            jax.ShapeDtypeStruct((2, *lists.shape), jnp.int32),
            jax.ShapeDtypeStruct((128, 128, 128), jnp.float32),
            jax.ShapeDtypeStruct((8, 128, 128), jnp.float32),
        ),
        in_specs=[
            pl.BlockSpec(memory_space=pltpu.HBM),
            pl.BlockSpec(memory_space=pltpu.HBM),
            pl.BlockSpec(memory_space=pltpu.VMEM),
        ],
        out_specs=(
            pl.BlockSpec(memory_space=space),
            pl.BlockSpec(memory_space=space),
            pl.BlockSpec(memory_space=pltpu.VMEM),
            pl.BlockSpec(memory_space=pltpu.VMEM),
            pl.BlockSpec(memory_space=pltpu.VMEM),
        ),
        scratch_shapes=[
            pltpu.SemaphoreType.DMA((3,)),
            pltpu.SemaphoreType.DMA((GATHER_COPIES,)),
            pltpu.SemaphoreType.DMA((GATHER_COPIES,)),
        ],
        compiler_params=pltpu.CompilerParams(
            collective_id=0, has_side_effects=True, vmem_limit_bytes=8 * 2**20
        ),
    )(
        pltpu.with_memory_space_constraint(user_factors.reshape(2, 4, 128, 128), pltpu.HBM),
        pltpu.with_memory_space_constraint(ratings, pltpu.HBM),
        lists,
    )


GROUP = 16


def local_kernel(core, lists, users, items, ratings, no_users, no_items, user_sum, item_sum, order):
    mine = core[0]

    def scan(table):
        live = lists[table, 2, 0]

        def visit(eight, count):
            for k in range(8):
                slot = eight * 8 + k
                block = lists[table, 0, slot]
                order[count] = ((table * 128 + slot) << 11) | (block << 3) | lists[table, 1, slot]
                keep = (((block >> 3) & 1) == mine) & (slot < live)
                count = count + keep.astype(jnp.int32)
            return count

        return lambda count: lax.fori_loop(0, (live + 7) >> 3, visit, count)

    count = scan(1)(scan(0)(jnp.int32(0)))
    for k in range(GROUP):
        order[count + k] = 0

    def step(g, carry):
        first = g * GROUP
        records = []
        for k in range(GROUP):
            n = first + k
            entry = order[n]
            item = entry & 7
            tile = ((entry >> 7) & 15) * 8 + ((entry >> 3) & 7)
            user_tile = users[tile]
            item_tile = items[item]
            predicted = lax.dot_general(
                user_tile, item_tile, (((1,), (1,)), ((), ())), preferred_element_type=jnp.float32
            )
            scores = ratings[entry >> 11]
            floor = jnp.where(n < count, 0, 1 << 20)
            errors = jnp.where(
                scores > floor, predicted - (scores.astype(jnp.float32) - 3.0), 0.0
            ).astype(jnp.bfloat16)
            records.append((tile, item, user_tile, item_tile, errors))
        terms = []
        for tile, item, user_tile, item_tile, errors in records:
            user_term = jnp.dot(errors, item_tile, preferred_element_type=jnp.float32)
            item_term = lax.dot_general(
                errors, user_tile, (((0,), (0,)), ((), ())), preferred_element_type=jnp.float32
            )
            terms.append((tile, item, user_term, item_term))
        for tile, item, user_term, item_term in terms:
            user_sum[tile] += user_term
            item_sum[item] += item_term
        return carry

    lax.fori_loop(0, (count + GROUP - 1) // GROUP, step, 0)


def local(core, lists, users, items, ratings, no_users, no_items):
    smem = pl.BlockSpec(memory_space=pltpu.SMEM)
    vmem = pl.BlockSpec(memory_space=pltpu.VMEM)
    return pl.pallas_call(
        local_kernel,
        out_shape=(
            jax.ShapeDtypeStruct((128, 128, 128), jnp.float32),
            jax.ShapeDtypeStruct((8, 128, 128), jnp.float32),
        ),
        in_specs=[smem, smem, vmem, vmem, vmem, vmem, vmem],
        out_specs=(vmem, vmem),
        input_output_aliases={5: 0, 6: 1},
        scratch_shapes=[pltpu.SMEM((256 + GROUP,), jnp.int32)],
        compiler_params=pltpu.CompilerParams(vmem_limit_bytes=8 * 2**20),
    )(core, lists, users, items, ratings, no_users, no_items)


user_step = 0.1
item_step = 0.04
shrinkage = 0.1
EDGE_ROWS, MIDDLE_ROWS = 56, 16
CHUNK = 4 * EDGE_ROWS


def coded_rows(rows):
    return rows + (16 if rows % 16 == 0 else 8)


def encode(value, buffer):
    rows = value.shape[0]
    folded = value.reshape(rows // 8, 8, 128)
    peak = jnp.maximum(jnp.max(jnp.abs(folded), axis=0), 1e-30)
    power = jnp.ceil(jnp.log2(peak))
    whole = jnp.round(folded * jnp.exp2(14.0 - power)).reshape(rows, 128)
    tail = [power] * ((coded_rows(rows) - rows) // 8)
    buffer[...] = jnp.concatenate([whole, *tail], axis=0).astype(jnp.int32).astype(jnp.int16)


def decode(buffer, rows):
    every = coded_rows(rows)
    power = buffer[every - 16:every].astype(jnp.float32)[8:16]
    folded = buffer[...].astype(jnp.float32)[0:rows].reshape(rows // 8, 8, 128)
    return (folded * jnp.exp2(power - 14.0)).reshape(rows, 128)


def reduce_kernel(
    sums, item_sums, own_users, own_items, new_users, new_items,
    half_out, half_in, near_out, near_in, far_out, far_in, column_out, column_in, total,
    last_out, last_in, grads,
    mid_far_out, mid_far_in, mid_out, mid_in, mid_total, mid_y_out, mid_y_in, mid_row, mid_x_out, mid_x_in, mid_grads,
    item_in, item_half, item_pair_out, item_pair_in, item_row, item_out, item_z, item_grads,
    half_send, half_recv, near_send, near_recv, far_send, far_recv, column_send, column_recv,
    last_send, last_recv, grad_send, grad_recv,
    mid_far_send, mid_far_recv, mid_send, mid_recv, mid_y_send, mid_y_recv, mid_x_send, mid_x_recv,
    mid_grad_send, mid_grad_recv,
    item_send, item_recv, item_z_send, item_z_recv, item_back_send, item_back_recv,
):
    z, ylo, yhi, x, c = here()
    y = yhi * 2 + ylo
    q = yhi * 4 + x

    def turn(v, k, n):
        return lax.rem(v + k, n)

    def copy(src, dst, send_sem, recv_sem, where):
        return pltpu.make_async_remote_copy(
            src_ref=src, dst_ref=dst, send_sem=send_sem, recv_sem=recv_sem,
            device_id=where, device_id_type=MESH,
        )

    def offset_of(i):
        return 4 + (1 - 2 * lax.rem(i, 2)) * ((i + 1) // 2)

    barrier = pltpu.get_barrier_semaphore()
    others = [device(z, y, turn(x, k, 4), c) for k in (1, 3)]
    others += [device(z, turn(y, k, 4), x, c) for k in (1, 3)]
    others += [device(turn(z, k, 8), y, x, c) for k in (1, 7)]
    others += [device(z, y, x, 1 - c)]
    for other in others:
        pl.semaphore_signal(barrier, inc=1, device_id=other, device_id_type=MESH)
    pl.semaphore_wait(barrier, len(others))

    mate = device(z, y, x, 1 - c)
    pair = device(z, yhi * 2 + 1 - ylo, x, c)
    item_first = copy(item_sums.at[pl.ds((1 - c) * 4, 4)], item_in, item_send.at[0], item_recv.at[0], mate)
    item_first.start()

    def plane_where(part, k):
        return device(z, y, turn(x, k, 4), c) if part == 0 else device(z, turn(y, k, 4), x, c)

    def plane_block(part, zz, k):
        if part == 0:
            return sums[zz, :, :, turn(x, k, 4), 0:EDGE_ROWS].reshape(CHUNK, 128)
        other = turn(y, k, 4)
        return sums[zz, lax.rem(other, 2), other // 2, :, EDGE_ROWS:2 * EDGE_ROWS].reshape(CHUNK, 128)

    def toward(part, way):
        return plane_where(part, 1 if way == 0 else 3)

    def half_copy(part, i, way):
        return copy(
            half_out.at[part, i, way], half_in.at[part, i, way],
            half_send.at[part, i, way], half_recv.at[part, i, way], toward(part, way),
        )

    def near_copy(part, i, way):
        return copy(
            near_out.at[part, i, way], near_in.at[part, i, way],
            near_send.at[part, i, way], near_recv.at[part, i, way], toward(part, way),
        )

    def add_half(value, way, extra):
        split = value.shape[0] // 2
        if way == 0:
            return jnp.concatenate([value[0:split] + extra, value[split:]], axis=0)
        return jnp.concatenate([value[0:split], value[split:] + extra], axis=0)

    def half_step(i, carry):
        zz = turn(z, offset_of(i), 8)
        for way in (0, 1):
            for part in (0, 1):
                block = plane_block(part, zz, 2)[CHUNK // 2 * way:CHUNK // 2 * (way + 1)]
                encode(block, half_out.at[part, i, way])
                half_copy(part, i, way).start()
        return carry

    def near_step(i, carry):
        zz = turn(z, offset_of(i), 8)
        for way in (0, 1):
            for part in (0, 1):
                half_copy(part, i, way).wait_recv()
                block = plane_block(part, zz, 1 if way == 0 else 3)
                block = add_half(block, way, decode(half_in.at[part, i, way], CHUNK // 2))
                encode(block, near_out.at[part, i, way])
                near_copy(part, i, way).start()
        return carry

    def plane_total(i):
        zz = turn(z, offset_of(i), 8)
        for part in (0, 1):
            for way in (0, 1):
                near_copy(part, i, way).wait_recv()
            value = plane_block(part, zz, 0)
            for way in (0, 1):
                value += decode(near_in.at[part, i, way], CHUNK)
            total[part, lax.rem(i, 2)] = value

    def z_where(way):
        return device(turn(z, 1 + 6 * way, 8), y, x, c)

    def far_copy(part, way):
        return copy(
            far_out.at[part, way], far_in.at[part, way], far_send.at[part, way], far_recv.at[part, way],
            z_where(way),
        )

    def column_copy(part, distance, way):
        return copy(
            column_out.at[part, distance - 1, way], column_in.at[part, distance - 1, way],
            column_send.at[part, distance - 1, way], column_recv.at[part, distance - 1, way],
            z_where(way),
        )

    def far_step():
        for part in (0, 1):
            for way in (0, 1):
                encode(total[part, 0, CHUNK // 2 * way:CHUNK // 2 * (way + 1)], far_out.at[part, way])
                far_copy(part, way).start()

    def third_step(way):
        for part in (0, 1):
            far_copy(part, way).wait_recv()
            value = add_half(total[part, 1 - way], way, decode(far_in.at[part, way], CHUNK // 2))
            encode(value, column_out.at[part, 2, way])
            column_copy(part, 3, way).start()

    def column_step(i):
        way = 1 - lax.rem(i, 2)
        distance = 4 - (i + 1) // 2
        for part in (0, 1):
            column_copy(part, distance + 1, way).wait_recv()
            value = total[part, lax.rem(i, 2)] + decode(column_in.at[part, distance, way], CHUNK)
            encode(value, column_out.at[part, distance - 1, way])
            column_copy(part, distance, way).start()

    def both_step(i, carry):
        plane_total(i)
        column_step(i - 1)
        return carry

    def mid_block(zz):
        return sums[zz, :, :, :, 2 * EDGE_ROWS:128].reshape(16 * MIDDLE_ROWS, 128)

    def mid_far_copy(way):
        return copy(
            mid_far_out.at[way], mid_far_in.at[way], mid_far_send.at[way], mid_far_recv.at[way], z_where(way)
        )

    def mid_copy(distance, way):
        return copy(
            mid_out.at[distance - 1, way], mid_in.at[distance - 1, way],
            mid_send.at[distance - 1, way], mid_recv.at[distance - 1, way], z_where(way),
        )

    def mid_far():
        for way in (0, 1):
            block = mid_block(turn(z, 4, 8))[8 * MIDDLE_ROWS * way:8 * MIDDLE_ROWS * (way + 1)]
            encode(block, mid_far_out.at[way])
            mid_far_copy(way).start()

    def mid_step(distance):
        for way in (0, 1):
            block = mid_block(turn(z, distance if way == 0 else 8 - distance, 8))
            if distance == 3:
                mid_far_copy(way).wait_recv()
                block = add_half(block, way, decode(mid_far_in.at[way], 8 * MIDDLE_ROWS))
            else:
                mid_copy(distance + 1, way).wait_recv()
                block += decode(mid_in.at[distance, way], 16 * MIDDLE_ROWS)
            encode(block, mid_out.at[distance - 1, way])
            mid_copy(distance, way).start()

    def mid_y_copy(k):
        return copy(
            mid_y_out.at[k - 1], mid_y_in.at[k - 1], mid_y_send.at[k - 1], mid_y_recv.at[k - 1],
            plane_where(1, k),
        )

    def mid_x_copy(k):
        return copy(
            mid_x_out.at[k - 1], mid_x_in.at[k - 1], mid_x_send.at[k - 1], mid_x_recv.at[k - 1],
            plane_where(0, k),
        )

    def mid_y_rows(k):
        other = turn(y, k, 4)
        place = lax.rem(other, 2) * 2 + other // 2
        size = 4 * MIDDLE_ROWS
        return mid_total[pl.ds(pl.multiple_of(place * size, size), size)]

    def mid_x_rows(k):
        return mid_row[pl.ds(pl.multiple_of(turn(x, k, 4) * MIDDLE_ROWS, MIDDLE_ROWS), MIDDLE_ROWS)]

    def mid_to_y():
        value = mid_block(z)
        for way in (0, 1):
            mid_copy(1, way).wait_recv()
            value += decode(mid_in.at[0, way], 16 * MIDDLE_ROWS)
        mid_total[...] = value
        for k in (2, 1, 3):
            encode(mid_y_rows(k), mid_y_out.at[k - 1])
            mid_y_copy(k).start()

    def mid_to_x():
        value = mid_y_rows(0)
        for k in (1, 2, 3):
            mid_y_copy(k).wait_recv()
            value += decode(mid_y_in.at[k - 1], 4 * MIDDLE_ROWS)
        mid_row[...] = value
        for k in (2, 1, 3):
            encode(mid_x_rows(k), mid_x_out.at[k - 1])
            mid_x_copy(k).start()

    def q_where(m):
        other = turn(q, m, 8)
        return device(z, (other // 4) * 2 + ylo, lax.rem(other, 4), c)

    def mid_grad_copy(m):
        return copy(
            mid_grads.at[q], mid_grads.at[q], mid_grad_send.at[m - 1], mid_grad_recv.at[m - 1], q_where(m)
        )

    def mid_finish():
        value = mid_x_rows(0)
        for k in (1, 2, 3):
            mid_x_copy(k).wait_recv()
            value += decode(mid_x_in.at[k - 1], MIDDLE_ROWS)
        encode(value, mid_grads.at[q])
        for m in range(1, 8):
            mid_grad_copy(m).start()

    item_pair = copy(item_pair_out, item_pair_in, item_send.at[1], item_recv.at[1], pair)

    def item_to_pair():
        item_first.wait_recv()
        item_half[...] = item_sums[pl.ds(c * 4, 4)].reshape(512, 128) + item_in[...].reshape(512, 128)
        encode(item_half[pl.ds(pl.multiple_of((1 - ylo) * 256, 256), 256)], item_pair_out)
        item_pair.start()

    def item_z_copy(o):
        return copy(
            item_out.at[o - 1], item_z.at[o - 1], item_z_send.at[o - 1], item_z_recv.at[o - 1],
            device(turn(z, o, 8), y, x, c),
        )

    def item_rows(zz):
        return item_row[pl.ds(pl.multiple_of(zz * 32, 32), 32)]

    def item_to_z():
        item_pair.wait_recv()
        own = item_half[pl.ds(pl.multiple_of(ylo * 256, 256), 256)]
        item_row[...] = own + decode(item_pair_in, 256)

        def each(o, carry):
            encode(item_rows(turn(z, o, 8)), item_out.at[o - 1])
            item_z_copy(o).start()
            return carry

        lax.fori_loop(1, 8, each, 0)

    def item_back(o):
        return copy(
            item_grads.at[c, ylo, z], item_grads.at[c, ylo, z], item_back_send.at[o - 1], item_back_recv.at[o - 1],
            device(turn(z, o, 8), y, x, c),
        )

    def item_total():
        def each(o, value):
            item_z_copy(o).wait_recv()
            return value + decode(item_z.at[o - 1], 32)

        encode(lax.fori_loop(1, 8, each, item_rows(z)), item_grads.at[c, ylo, z])

        def start(o, carry):
            item_back(o).start()
            return carry

        lax.fori_loop(1, 8, start, 0)

    item_share = copy(
        item_grads.at[c, ylo], item_grads.at[c, ylo], item_send.at[2], item_recv.at[2], pair
    )
    item_last = copy(item_grads.at[c], item_grads.at[c], item_send.at[3], item_recv.at[3], mate)

    def item_to_share():
        def each(o, carry):
            item_back(o).wait_recv()
            return carry

        lax.fori_loop(1, 8, each, 0)
        item_share.start()

    def last_rows(part, k):
        if part == 0:
            other = turn(y, k, 4)
            place = lax.rem(other, 2) * 2 + other // 2
        else:
            place = turn(x, k, 4)
        return total[part, 1, pl.ds(pl.multiple_of(place * EDGE_ROWS, 8), EDGE_ROWS)]

    def last_copy(part, k):
        return copy(
            last_out.at[part, k - 1], last_in.at[part, k - 1],
            last_send.at[part, k - 1], last_recv.at[part, k - 1], plane_where(1 - part, k),
        )

    def grad_copy(m):
        return copy(grads.at[q], grads.at[q], grad_send.at[m - 1], grad_recv.at[m - 1], q_where(m))

    mid_far()
    lax.fori_loop(0, 8, half_step, 0)
    item_to_pair()
    mid_step(3)
    lax.fori_loop(0, 4, near_step, 0)
    mid_step(2)
    lax.fori_loop(4, 8, near_step, 0)
    plane_total(0)
    mid_step(1)
    plane_total(1)
    far_step()
    plane_total(2)
    third_step(0)
    mid_to_y()
    plane_total(3)
    third_step(1)
    item_to_z()
    lax.fori_loop(4, 6, both_step, 0)
    mid_to_x()
    both_step(6, 0)
    column_step(6)
    item_total()
    mid_finish()
    plane_total(7)
    for part in (0, 1):
        for way in (0, 1):
            column_copy(part, 1, way).wait_recv()
            total[part, 1] += decode(column_in.at[part, 0, way], CHUNK)
    for k in (2, 1, 3):
        for part in (0, 1):
            encode(last_rows(part, k), last_out.at[part, k - 1])
            last_copy(part, k).start()
    item_to_share()
    halves = []
    for part in (0, 1):
        value = last_rows(part, 0)
        for k in (1, 2, 3):
            last_copy(part, k).wait_recv()
            value += decode(last_in.at[part, k - 1], EDGE_ROWS)
        halves.append(value)
    encode(jnp.concatenate(halves, axis=0), grads.at[q])
    for m in range(1, 8):
        grad_copy(m).start()
    item_share.wait_recv()
    item_last.start()

    def plane_drain(i, carry):
        for part in (0, 1):
            for way in (0, 1):
                half_copy(part, i, way).wait_send()
                near_copy(part, i, way).wait_send()
        return carry

    def peer_drain(o, carry):
        item_z_copy(o).wait_send()
        item_back(o).wait_send()
        mid_grad_copy(o).wait_send()
        return carry

    lax.fori_loop(0, 8, plane_drain, 0)
    lax.fori_loop(1, 8, peer_drain, 0)
    for way in (0, 1):
        mid_far_copy(way).wait_send()
        for part in (0, 1):
            far_copy(part, way).wait_send()
        for distance in (1, 2, 3):
            mid_copy(distance, way).wait_send()
            for part in (0, 1):
                column_copy(part, distance, way).wait_send()
    for k in (1, 2, 3):
        mid_y_copy(k).wait_send()
        mid_x_copy(k).wait_send()
        for part in (0, 1):
            last_copy(part, k).wait_send()
    item_last.wait_recv()

    def item_finish(n, carry):
        grad = decode(item_grads.at[n // 16, lax.rem(n // 8, 2), lax.rem(n, 8)], 32)
        rows = pl.ds(pl.multiple_of(n * 32, 32), 32)
        now = own_items[rows].astype(jnp.float32)
        new_items[rows] = now - item_step * (grad + shrinkage * now)
        return carry

    lax.fori_loop(0, 32, item_finish, 0)
    for m in range(1, 8):
        mid_grad_copy(m).wait_recv()
    for m in range(1, 8):
        grad_copy(m).wait_recv()

    def user_finish(j, carry):
        grad = jnp.concatenate(
            [decode(grads.at[j], 2 * EDGE_ROWS), decode(mid_grads.at[j], MIDDLE_ROWS)], axis=0
        )
        rows = pl.ds(pl.multiple_of(j * 128, 128), 128)
        now = own_users[rows].astype(jnp.float32)
        new_users[rows] = now - user_step * (grad + shrinkage * now)
        return carry

    lax.fori_loop(0, 8, user_finish, 0)
    for m in range(1, 8):
        grad_copy(m).wait_send()
    for early in (item_first, item_pair, item_share, item_last):
        early.wait_send()


def reduce(sums, item_sums, own_users, own_items):
    vmem = pl.BlockSpec(memory_space=pltpu.VMEM)
    dma = pltpu.SemaphoreType.DMA
    i16, f32 = jnp.int16, jnp.float32
    half = (2, 8, 2, coded_rows(CHUNK // 2), 128)
    near = (2, 8, 2, coded_rows(CHUNK), 128)
    far = (2, 2, coded_rows(CHUNK // 2), 128)
    column = (2, 3, 2, coded_rows(CHUNK), 128)
    last = (2, 3, coded_rows(EDGE_ROWS), 128)
    mid_far = (2, coded_rows(8 * MIDDLE_ROWS), 128)
    mid = (3, 2, coded_rows(16 * MIDDLE_ROWS), 128)
    mid_y = (3, coded_rows(4 * MIDDLE_ROWS), 128)
    mid_x = (3, coded_rows(MIDDLE_ROWS), 128)
    item_z = (7, coded_rows(32), 128)
    item_pair = (coded_rows(256), 128)
    both = lambda shape: [pltpu.VMEM(shape, i16)] * 2
    sems = lambda *shape: [dma(shape)] * 2
    return pl.pallas_call(
        reduce_kernel,
        out_shape=(
            jax.ShapeDtypeStruct((1024, 128), f32),
            jax.ShapeDtypeStruct((1024, 128), f32),
        ),
        in_specs=[vmem, vmem, vmem, vmem],
        out_specs=(vmem, vmem),
        scratch_shapes=[
            *both(half), *both(near), *both(far), *both(column),
            pltpu.VMEM((2, 2, CHUNK, 128), f32),
            *both(last),
            pltpu.VMEM((8, coded_rows(2 * EDGE_ROWS), 128), i16),
            *both(mid_far), *both(mid),
            pltpu.VMEM((16 * MIDDLE_ROWS, 128), f32),
            *both(mid_y),
            pltpu.VMEM((4 * MIDDLE_ROWS, 128), f32),
            *both(mid_x),
            pltpu.VMEM((8, coded_rows(MIDDLE_ROWS), 128), i16),
            pltpu.VMEM((4, 128, 128), f32), pltpu.VMEM((512, 128), f32),
            *both(item_pair),
            pltpu.VMEM((256, 128), f32),
            *both(item_z),
            pltpu.VMEM((2, 2, 8, coded_rows(32), 128), i16),
            *sems(2, 8, 2), *sems(2, 8, 2), *sems(2, 2), *sems(2, 3, 2),
            *sems(2, 3), *sems(7),
            *sems(2), *sems(3, 2), *sems(3), *sems(3), *sems(7),
            *sems(4), *sems(7), *sems(7),
        ],
        compiler_params=pltpu.CompilerParams(
            collective_id=1, has_side_effects=True, vmem_limit_bytes=16 * 2**20
        ),
    )(sums.reshape(8, 2, 2, 4, 128, 128), item_sums, own_users, own_items)


def body(user_factors, item_factors, block_user, block_item, live_blocks, ratings):
    slots = ratings.shape[2]
    scores = ratings.reshape(slots, 128, 128)
    lists = jnp.concatenate(
        [
            block_user.reshape(1, slots),
            block_item.reshape(1, slots),
            jnp.broadcast_to(live_blocks.reshape(1, 1), (1, slots)),
            jnp.zeros((5, slots), jnp.int32),
        ],
        axis=0,
    )
    users, all_scores, all_lists, no_users, no_items = gather(user_factors, scores, lists)
    core = lax.rem(lax.axis_index("user"), 2).astype(jnp.int32).reshape(1)
    user_sums, item_sums = local(
        core, all_lists, users.reshape(128, 128, 128), item_factors.reshape(8, 128, 128),
        all_scores.reshape(256, 128, 128), no_users, no_items,
    )
    return reduce(user_sums, item_sums, user_factors, item_factors)


def solution(mesh):
    return jax.shard_map(
        body,
        mesh=mesh,
        in_specs=(
            P("user", None),
            P("item", None),
            P("user", "item", None),
            P("user", "item", None),
            P("user", "item"),
            P("user", "item", None, None, None),
        ),
        out_specs=(P("user", None), P("item", None)),
        check_vma=False,
    )
```

```python
import functools

import jax
import jax.numpy as jnp
from jax import lax
from jax.experimental import pallas as pl
from jax.experimental.pallas import tpu as pltpu
from jax.sharding import PartitionSpec as P

MESH = pl.DeviceIdType.MESH


def here():
    p = lax.axis_index("user")
    q = lax.axis_index("item")
    return p // 4, lax.rem(p // 2, 2), q // 4, lax.rem(q, 4), lax.rem(p, 2)


def device(z, y, x, c):
    return (z * 4 + lax.rem(y, 2) * 2 + c, (y // 2) * 4 + x)


def neighbours():
    z, ylo, yhi, x, c = here()
    y = yhi * 2 + ylo
    up = lambda v, n: lax.rem(v + 1, n)
    down = lambda v, n: lax.rem(v + n - 1, n)
    return {
        "x": (device(z, y, up(x, 4), c), device(z, y, down(x, 4), c)),
        "y": (device(z, up(y, 4), x, c), device(z, down(y, 4), x, c)),
        "z": (device(up(z, 8), y, x, c), device(down(z, 8), y, x, c)),
        "pair": device(z, yhi * 2 + 1 - ylo, x, c),
        "mate": device(z, y, x, 1 - c),
    }


def meet(near):
    barrier = pltpu.get_barrier_semaphore()
    others = [*near["x"], *near["y"], *near["z"], near["mate"]]
    for other in others:
        pl.semaphore_signal(barrier, inc=1, device_id=other, device_id_type=MESH)
    pl.semaphore_wait(barrier, len(others))


class Sender:
    def __init__(self, send_sems, recv_sems):
        self.send_sems, self.recv_sems, self.used, self.copies = send_sems, recv_sems, 0, []

    def __call__(self, src, dst, where):
        copy = pltpu.make_async_remote_copy(
            src_ref=src,
            dst_ref=dst,
            send_sem=self.send_sems.at[self.used],
            recv_sem=self.recv_sems.at[self.used],
            device_id=where,
            device_id_type=MESH,
        )
        copy.start()
        self.used += 1
        self.copies.append(copy)
        return copy

    def drain(self):
        for copy in self.copies:
            copy.wait_send()


ROWS_A, ROWS_B, ROWS_C = 48, 48, 32
GATHER_COPIES = 160


def gather_kernel(split, own, ratings, lists, users, all_ratings, all_lists, no_users, no_items, local_sems, send_sems, recv_sems):
    z, ylo, yhi, x, c = here()
    y = yhi * 2 + ylo
    near = neighbours()
    keep = pltpu.make_async_copy(own, users.at[z, ylo], local_sems.at[0])
    keep.start()
    near_lists = pltpu.make_async_copy(lists, all_lists.at[c], local_sems.at[1])
    near_lists.start()
    near_ratings = pltpu.make_async_copy(ratings, all_ratings.at[c], local_sems.at[2])
    near_ratings.start()
    meet(near)
    send = Sender(send_sems, recv_sems)
    keep.wait()
    rows_a = pl.ds(0, split[0])
    rows_b = pl.ds(split[0], split[1])
    rows_c = pl.ds(split[0] + split[1], split[2])

    def zed(offset):
        return lax.rem(z + offset + 8, 8)

    def part_a(zz, low, xx, half=None):
        if half is None:
            return users.at[zz, low, :, xx, rows_a]
        return users.at[zz, low, half, xx, rows_a]

    def part_b(zz, yy, half=None):
        if half is None:
            return users.at[zz, lax.rem(yy, 2), yy // 2, :, rows_b]
        return users.at[zz, lax.rem(yy, 2), yy // 2, pl.ds(2 * half, 2), rows_b]

    def part_c(zz, low, half=None):
        if half is None:
            return users.at[zz, low, :, :, rows_c]
        return users.at[zz, low, half, :, rows_c]

    parts = {
        "A": lambda zz, half=None: part_a(zz, ylo, x, half),
        "B": lambda zz, half=None: part_b(zz, y, half),
        "C": lambda zz, half=None: part_c(zz, ylo, half),
        "D": lambda zz, half=None: part_c(zz, 1 - ylo, half),
    }
    along_z, pair, first, last = {}, {}, {}, []

    def z_send(name, step):
        for way in (0, 1):
            offset = -(step - 1) if way == 0 else step - 1
            block = parts[name](zed(offset), way if step == 4 else None)
            along_z[name, step, way] = send(block, block, near["z"][way])

    def z_wait(name, step):
        for way in (0, 1):
            along_z[name, step, way].wait_recv()

    def pair_send(offset):
        block = part_a(zed(offset), ylo, x)
        pair[offset] = send(block, block, near["pair"])

    late = (-3, 3, 4)

    def direct(block, where):
        last.append(send(block, block, where))

    def x_send(offset, low):
        if offset == 0 and low == 0 or offset == 4 and low == 1:
            return
        if offset in late:
            block = part_a(zed(offset), ylo if low == 0 else 1 - ylo, x)
            rows = (y, yhi * 2 + 1 - ylo) if offset == 4 else (y,)
            for k in (2, 1, 3):
                for row in rows:
                    direct(block, device(z, row, lax.rem(x + k, 4), c))
            return
        block = part_a(zed(offset), ylo if low == 0 else 1 - ylo, x)
        first["x", offset, low] = [send(block, block, near["x"][way]) for way in (0, 1)]

    def y_send(offset):
        if offset == 4:
            block = part_b(zed(offset), y)
            for k in (2, 1, 3):
                direct(block, device(z, lax.rem(y + k, 4), x, c))
            return
        block = part_b(zed(offset), y)
        first["y", offset, 0] = [send(block, block, near["y"][way]) for way in (0, 1)]

    def forward(axis, offset, low):
        zz = zed(offset)
        if axis == "x" and (offset == 0 and low == 0 or offset in late) or offset == 4:
            return
        for way in (0, 1):
            first[axis, offset, low][way].wait_recv()
            if axis == "y" and offset == 0:
                continue
            back = 3 if way == 0 else 1
            if axis == "x":
                block = part_a(zz, ylo if low == 0 else 1 - ylo, lax.rem(x + back, 4), way)
            else:
                block = part_b(zz, lax.rem(y + back, 4), way)
            last.append(send(block, block, near[axis][way]))

    z_send("A", 1)
    z_send("B", 1)
    pair_c = send(part_c(z, ylo), part_c(z, ylo), near["pair"])
    pair_send(0)
    z_send("C", 1)
    x_send(0, 0)
    y_send(0)
    far = send(ratings, all_ratings.at[c], near["mate"])
    far_lists = send(lists, all_lists.at[c], near["mate"])
    no_items[...] = jnp.zeros_like(no_items)

    def clear(k, carry):
        no_users[k] = jnp.zeros(no_users.shape[1:], jnp.float32)
        return carry

    lax.fori_loop(0, no_users.shape[0], clear, 0)
    before = [0]
    for step in (1, 2, 3, 4):
        offsets = [-step, step] if step < 4 else [4]
        z_wait("A", step)
        if step < 4:
            z_send("A", step + 1)
        z_wait("B", step)
        if step < 4:
            z_send("B", step + 1)
        for offset in offsets:
            pair_send(offset)
            x_send(offset, 0)
            y_send(offset)
        if step == 1:
            pair_c.wait_recv()
            z_send("D", 1)
        z_wait("C", step)
        if step < 4:
            z_send("C", step + 1)
        for offset in before:
            pair[offset].wait_recv()
            x_send(offset, 1)
        for offset in before:
            forward("y", offset, 0)
            forward("x", offset, 0)
        if step > 1:
            z_wait("D", step - 1)
            z_send("D", step)
            for offset in earlier:
                forward("x", offset, 1)
        earlier, before = before, offsets
    for offset in before:
        pair[offset].wait_recv()
        x_send(offset, 1)
    for offset in before:
        forward("y", offset, 0)
        forward("x", offset, 0)
    for offset in earlier + before:
        forward("x", offset, 1)
    z_wait("D", 4)
    for copy in last:
        copy.wait_recv()
    near_lists.wait()
    near_ratings.wait()
    far.wait_recv()
    far_lists.wait_recv()
    send.drain()


def gather(user_factors, ratings, lists, vmem=True):
    space = pltpu.VMEM if vmem else pl.ANY
    return pl.pallas_call(
        functools.partial(gather_kernel, (ROWS_A, ROWS_B, ROWS_C)),
        out_shape=(
            jax.ShapeDtypeStruct((8, 2, 2, 4, 128, 128), jnp.bfloat16),
            jax.ShapeDtypeStruct((2, *ratings.shape), jnp.int32),
            jax.ShapeDtypeStruct((2, *lists.shape), jnp.int32),
            jax.ShapeDtypeStruct((128, 128, 128), jnp.float32),
            jax.ShapeDtypeStruct((8, 128, 128), jnp.float32),
        ),
        in_specs=[
            pl.BlockSpec(memory_space=pltpu.HBM),
            pl.BlockSpec(memory_space=pltpu.HBM),
            pl.BlockSpec(memory_space=pltpu.VMEM),
        ],
        out_specs=(
            pl.BlockSpec(memory_space=space),
            pl.BlockSpec(memory_space=space),
            pl.BlockSpec(memory_space=pltpu.VMEM),
            pl.BlockSpec(memory_space=pltpu.VMEM),
            pl.BlockSpec(memory_space=pltpu.VMEM),
        ),
        scratch_shapes=[
            pltpu.SemaphoreType.DMA((3,)),
            pltpu.SemaphoreType.DMA((GATHER_COPIES,)),
            pltpu.SemaphoreType.DMA((GATHER_COPIES,)),
        ],
        compiler_params=pltpu.CompilerParams(
            collective_id=0, has_side_effects=True, vmem_limit_bytes=8 * 2**20
        ),
    )(
        pltpu.with_memory_space_constraint(user_factors.reshape(2, 4, 128, 128), pltpu.HBM),
        pltpu.with_memory_space_constraint(ratings, pltpu.HBM),
        lists,
    )


GROUP = 16


def local_kernel(core, lists, users, items, ratings, no_users, no_items, user_sum, item_sum, order):
    mine = core[0]

    def scan(table):
        live = lists[table, 2, 0]

        def visit(eight, count):
            for k in range(8):
                slot = eight * 8 + k
                block = lists[table, 0, slot]
                order[count] = ((table * 128 + slot) << 11) | (block << 3) | lists[table, 1, slot]
                keep = (((block >> 3) & 1) == mine) & (slot < live)
                count = count + keep.astype(jnp.int32)
            return count

        return lambda count: lax.fori_loop(0, (live + 7) >> 3, visit, count)

    count = scan(1)(scan(0)(jnp.int32(0)))
    for k in range(GROUP):
        order[count + k] = 0

    def step(g, carry):
        first = g * GROUP
        records = []
        for k in range(GROUP):
            n = first + k
            entry = order[n]
            item = entry & 7
            tile = ((entry >> 7) & 15) * 8 + ((entry >> 3) & 7)
            user_tile = users[tile]
            item_tile = items[item]
            predicted = lax.dot_general(
                user_tile, item_tile, (((1,), (1,)), ((), ())), preferred_element_type=jnp.float32
            )
            scores = ratings[entry >> 11]
            floor = jnp.where(n < count, 0, 1 << 20)
            errors = jnp.where(
                scores > floor, predicted - (scores.astype(jnp.float32) - 3.0), 0.0
            ).astype(jnp.bfloat16)
            records.append((tile, item, user_tile, item_tile, errors))
        terms = []
        for tile, item, user_tile, item_tile, errors in records:
            user_term = jnp.dot(errors, item_tile, preferred_element_type=jnp.float32)
            item_term = lax.dot_general(
                errors, user_tile, (((0,), (0,)), ((), ())), preferred_element_type=jnp.float32
            )
            terms.append((tile, item, user_term, item_term))
        for tile, item, user_term, item_term in terms:
            user_sum[tile] += user_term
            item_sum[item] += item_term
        return carry

    lax.fori_loop(0, (count + GROUP - 1) // GROUP, step, 0)


def local(core, lists, users, items, ratings, no_users, no_items):
    smem = pl.BlockSpec(memory_space=pltpu.SMEM)
    vmem = pl.BlockSpec(memory_space=pltpu.VMEM)
    return pl.pallas_call(
        local_kernel,
        out_shape=(
            jax.ShapeDtypeStruct((128, 128, 128), jnp.float32),
            jax.ShapeDtypeStruct((8, 128, 128), jnp.float32),
        ),
        in_specs=[smem, smem, vmem, vmem, vmem, vmem, vmem],
        out_specs=(vmem, vmem),
        input_output_aliases={5: 0, 6: 1},
        scratch_shapes=[pltpu.SMEM((256 + GROUP,), jnp.int32)],
        compiler_params=pltpu.CompilerParams(vmem_limit_bytes=8 * 2**20),
    )(core, lists, users, items, ratings, no_users, no_items)


user_step = 0.1
item_step = 0.04
shrinkage = 0.1
EDGE_ROWS, MIDDLE_ROWS = 56, 16
CHUNK = 4 * EDGE_ROWS


def coded_rows(rows):
    return rows + (16 if rows % 16 == 0 else 8)


def encode(value, buffer):
    rows = value.shape[0]
    folded = value.reshape(rows // 8, 8, 128)
    peak = jnp.maximum(jnp.max(jnp.abs(folded), axis=0), 1e-30)
    power = jnp.ceil(jnp.log2(peak))
    whole = jnp.round(folded * jnp.exp2(14.0 - power)).reshape(rows, 128)
    tail = [power] * ((coded_rows(rows) - rows) // 8)
    buffer[...] = jnp.concatenate([whole, *tail], axis=0).astype(jnp.int32).astype(jnp.int16)


def decode(buffer, rows):
    every = coded_rows(rows)
    power = buffer[every - 16:every].astype(jnp.float32)[8:16]
    folded = buffer[...].astype(jnp.float32)[0:rows].reshape(rows // 8, 8, 128)
    return (folded * jnp.exp2(power - 14.0)).reshape(rows, 128)


def reduce_kernel(
    sums, item_sums, own_users, own_items, new_users, new_items,
    half_out, half_in, near_out, near_in, far_out, far_in, column_out, column_in, total,
    last_out, last_in, grads,
    mid_far_out, mid_far_in, mid_out, mid_in, mid_total, mid_y_out, mid_y_in, mid_row, mid_x_out, mid_x_in, mid_grads,
    item_in, item_half, item_pair_out, item_pair_in, item_row, item_out, item_z, item_grads,
    half_send, half_recv, near_send, near_recv, far_send, far_recv, column_send, column_recv,
    last_send, last_recv, grad_send, grad_recv,
    mid_far_send, mid_far_recv, mid_send, mid_recv, mid_y_send, mid_y_recv, mid_x_send, mid_x_recv,
    mid_grad_send, mid_grad_recv,
    item_send, item_recv, item_z_send, item_z_recv, item_back_send, item_back_recv,
):
    z, ylo, yhi, x, c = here()
    y = yhi * 2 + ylo
    q = yhi * 4 + x

    def turn(v, k, n):
        return lax.rem(v + k, n)

    def copy(src, dst, send_sem, recv_sem, where):
        return pltpu.make_async_remote_copy(
            src_ref=src, dst_ref=dst, send_sem=send_sem, recv_sem=recv_sem,
            device_id=where, device_id_type=MESH,
        )

    def offset_of(i):
        return 4 + (1 - 2 * lax.rem(i, 2)) * ((i + 1) // 2)

    barrier = pltpu.get_barrier_semaphore()
    others = [device(z, y, turn(x, k, 4), c) for k in (1, 3)]
    others += [device(z, turn(y, k, 4), x, c) for k in (1, 3)]
    others += [device(turn(z, k, 8), y, x, c) for k in (1, 7)]
    others += [device(z, y, x, 1 - c)]
    for other in others:
        pl.semaphore_signal(barrier, inc=1, device_id=other, device_id_type=MESH)
    pl.semaphore_wait(barrier, len(others))

    mate = device(z, y, x, 1 - c)
    pair = device(z, yhi * 2 + 1 - ylo, x, c)
    item_first = copy(item_sums.at[pl.ds((1 - c) * 4, 4)], item_in, item_send.at[0], item_recv.at[0], mate)
    item_first.start()

    def plane_where(part, k):
        return device(z, y, turn(x, k, 4), c) if part == 0 else device(z, turn(y, k, 4), x, c)

    def plane_block(part, zz, k):
        if part == 0:
            return sums[zz, :, :, turn(x, k, 4), 0:EDGE_ROWS].reshape(CHUNK, 128)
        other = turn(y, k, 4)
        return sums[zz, lax.rem(other, 2), other // 2, :, EDGE_ROWS:2 * EDGE_ROWS].reshape(CHUNK, 128)

    def toward(part, way):
        return plane_where(part, 1 if way == 0 else 3)

    def half_copy(part, i, way):
        return copy(
            half_out.at[part, i, way], half_in.at[part, i, way],
            half_send.at[part, i, way], half_recv.at[part, i, way], toward(part, way),
        )

    def near_copy(part, i, way):
        return copy(
            near_out.at[part, i, way], near_in.at[part, i, way],
            near_send.at[part, i, way], near_recv.at[part, i, way], toward(part, way),
        )

    def add_half(value, way, extra):
        split = value.shape[0] // 2
        if way == 0:
            return jnp.concatenate([value[0:split] + extra, value[split:]], axis=0)
        return jnp.concatenate([value[0:split], value[split:] + extra], axis=0)

    def half_step(i, carry):
        zz = turn(z, offset_of(i), 8)
        for way in (0, 1):
            for part in (0, 1):
                block = plane_block(part, zz, 2)[CHUNK // 2 * way:CHUNK // 2 * (way + 1)]
                encode(block, half_out.at[part, i, way])
                half_copy(part, i, way).start()
        return carry

    def near_step(i, carry):
        zz = turn(z, offset_of(i), 8)
        for way in (0, 1):
            for part in (0, 1):
                half_copy(part, i, way).wait_recv()
                block = plane_block(part, zz, 1 if way == 0 else 3)
                block = add_half(block, way, decode(half_in.at[part, i, way], CHUNK // 2))
                encode(block, near_out.at[part, i, way])
                near_copy(part, i, way).start()
        return carry

    def plane_total(i):
        zz = turn(z, offset_of(i), 8)
        for part in (0, 1):
            for way in (0, 1):
                near_copy(part, i, way).wait_recv()
            value = plane_block(part, zz, 0)
            for way in (0, 1):
                value += decode(near_in.at[part, i, way], CHUNK)
            total[part, lax.rem(i, 2)] = value

    def z_where(way):
        return device(turn(z, 1 + 6 * way, 8), y, x, c)

    def far_copy(part, way):
        return copy(
            far_out.at[part, way], far_in.at[part, way], far_send.at[part, way], far_recv.at[part, way],
            z_where(way),
        )

    def column_copy(part, distance, way):
        return copy(
            column_out.at[part, distance - 1, way], column_in.at[part, distance - 1, way],
            column_send.at[part, distance - 1, way], column_recv.at[part, distance - 1, way],
            z_where(way),
        )

    def far_step():
        for part in (0, 1):
            for way in (0, 1):
                encode(total[part, 0, CHUNK // 2 * way:CHUNK // 2 * (way + 1)], far_out.at[part, way])
                far_copy(part, way).start()

    def third_step(way):
        for part in (0, 1):
            far_copy(part, way).wait_recv()
            value = add_half(total[part, 1 - way], way, decode(far_in.at[part, way], CHUNK // 2))
            encode(value, column_out.at[part, 2, way])
            column_copy(part, 3, way).start()

    def column_step(i):
        way = 1 - lax.rem(i, 2)
        distance = 4 - (i + 1) // 2
        for part in (0, 1):
            column_copy(part, distance + 1, way).wait_recv()
            value = total[part, lax.rem(i, 2)] + decode(column_in.at[part, distance, way], CHUNK)
            encode(value, column_out.at[part, distance - 1, way])
            column_copy(part, distance, way).start()

    def both_step(i, carry):
        plane_total(i)
        column_step(i - 1)
        return carry

    def mid_block(zz):
        return sums[zz, :, :, :, 2 * EDGE_ROWS:128].reshape(16 * MIDDLE_ROWS, 128)

    def mid_far_copy(way):
        return copy(
            mid_far_out.at[way], mid_far_in.at[way], mid_far_send.at[way], mid_far_recv.at[way], z_where(way)
        )

    def mid_copy(distance, way):
        return copy(
            mid_out.at[distance - 1, way], mid_in.at[distance - 1, way],
            mid_send.at[distance - 1, way], mid_recv.at[distance - 1, way], z_where(way),
        )

    def mid_far():
        for way in (0, 1):
            block = mid_block(turn(z, 4, 8))[8 * MIDDLE_ROWS * way:8 * MIDDLE_ROWS * (way + 1)]
            encode(block, mid_far_out.at[way])
            mid_far_copy(way).start()

    def mid_step(distance):
        for way in (0, 1):
            block = mid_block(turn(z, distance if way == 0 else 8 - distance, 8))
            if distance == 3:
                mid_far_copy(way).wait_recv()
                block = add_half(block, way, decode(mid_far_in.at[way], 8 * MIDDLE_ROWS))
            else:
                mid_copy(distance + 1, way).wait_recv()
                block += decode(mid_in.at[distance, way], 16 * MIDDLE_ROWS)
            encode(block, mid_out.at[distance - 1, way])
            mid_copy(distance, way).start()

    def mid_y_copy(k):
        return copy(
            mid_y_out.at[k - 1], mid_y_in.at[k - 1], mid_y_send.at[k - 1], mid_y_recv.at[k - 1],
            plane_where(1, k),
        )

    def mid_x_copy(k):
        return copy(
            mid_x_out.at[k - 1], mid_x_in.at[k - 1], mid_x_send.at[k - 1], mid_x_recv.at[k - 1],
            plane_where(0, k),
        )

    def mid_y_rows(k):
        other = turn(y, k, 4)
        place = lax.rem(other, 2) * 2 + other // 2
        size = 4 * MIDDLE_ROWS
        return mid_total[pl.ds(pl.multiple_of(place * size, size), size)]

    def mid_x_rows(k):
        return mid_row[pl.ds(pl.multiple_of(turn(x, k, 4) * MIDDLE_ROWS, MIDDLE_ROWS), MIDDLE_ROWS)]

    def mid_to_y():
        value = mid_block(z)
        for way in (0, 1):
            mid_copy(1, way).wait_recv()
            value += decode(mid_in.at[0, way], 16 * MIDDLE_ROWS)
        mid_total[...] = value
        for k in (2, 1, 3):
            encode(mid_y_rows(k), mid_y_out.at[k - 1])
            mid_y_copy(k).start()

    def mid_to_x():
        value = mid_y_rows(0)
        for k in (1, 2, 3):
            mid_y_copy(k).wait_recv()
            value += decode(mid_y_in.at[k - 1], 4 * MIDDLE_ROWS)
        mid_row[...] = value
        for k in (2, 1, 3):
            encode(mid_x_rows(k), mid_x_out.at[k - 1])
            mid_x_copy(k).start()

    def q_where(m):
        other = turn(q, m, 8)
        return device(z, (other // 4) * 2 + ylo, lax.rem(other, 4), c)

    def mid_grad_copy(m):
        return copy(
            mid_grads.at[q], mid_grads.at[q], mid_grad_send.at[m - 1], mid_grad_recv.at[m - 1], q_where(m)
        )

    def mid_finish():
        value = mid_x_rows(0)
        for k in (1, 2, 3):
            mid_x_copy(k).wait_recv()
            value += decode(mid_x_in.at[k - 1], MIDDLE_ROWS)
        encode(value, mid_grads.at[q])
        for m in range(1, 8):
            mid_grad_copy(m).start()

    item_pair = copy(item_pair_out, item_pair_in, item_send.at[1], item_recv.at[1], pair)

    def item_to_pair():
        item_first.wait_recv()
        item_half[...] = item_sums[pl.ds(c * 4, 4)].reshape(512, 128) + item_in[...].reshape(512, 128)
        encode(item_half[pl.ds(pl.multiple_of((1 - ylo) * 256, 256), 256)], item_pair_out)
        item_pair.start()

    def item_z_copy(o):
        return copy(
            item_out.at[o - 1], item_z.at[o - 1], item_z_send.at[o - 1], item_z_recv.at[o - 1],
            device(turn(z, o, 8), y, x, c),
        )

    def item_rows(zz):
        return item_row[pl.ds(pl.multiple_of(zz * 32, 32), 32)]

    def item_to_z():
        item_pair.wait_recv()
        own = item_half[pl.ds(pl.multiple_of(ylo * 256, 256), 256)]
        item_row[...] = own + decode(item_pair_in, 256)

        def each(o, carry):
            encode(item_rows(turn(z, o, 8)), item_out.at[o - 1])
            item_z_copy(o).start()
            return carry

        lax.fori_loop(1, 8, each, 0)

    def item_back(o):
        return copy(
            item_grads.at[c, ylo, z], item_grads.at[c, ylo, z], item_back_send.at[o - 1], item_back_recv.at[o - 1],
            device(turn(z, o, 8), y, x, c),
        )

    def item_total():
        def each(o, value):
            item_z_copy(o).wait_recv()
            return value + decode(item_z.at[o - 1], 32)

        encode(lax.fori_loop(1, 8, each, item_rows(z)), item_grads.at[c, ylo, z])

        def start(o, carry):
            item_back(o).start()
            return carry

        lax.fori_loop(1, 8, start, 0)

    item_share = copy(
        item_grads.at[c, ylo], item_grads.at[c, ylo], item_send.at[2], item_recv.at[2], pair
    )
    item_last = copy(item_grads.at[c], item_grads.at[c], item_send.at[3], item_recv.at[3], mate)

    def item_to_share():
        def each(o, carry):
            item_back(o).wait_recv()
            return carry

        lax.fori_loop(1, 8, each, 0)
        item_share.start()

    def last_rows(part, k):
        if part == 0:
            other = turn(y, k, 4)
            place = lax.rem(other, 2) * 2 + other // 2
        else:
            place = turn(x, k, 4)
        return total[part, 1, pl.ds(pl.multiple_of(place * EDGE_ROWS, 8), EDGE_ROWS)]

    def last_copy(part, k):
        return copy(
            last_out.at[part, k - 1], last_in.at[part, k - 1],
            last_send.at[part, k - 1], last_recv.at[part, k - 1], plane_where(1 - part, k),
        )

    def grad_copy(m):
        return copy(grads.at[q], grads.at[q], grad_send.at[m - 1], grad_recv.at[m - 1], q_where(m))

    mid_far()
    lax.fori_loop(0, 8, half_step, 0)
    item_to_pair()
    mid_step(3)
    lax.fori_loop(0, 4, near_step, 0)
    mid_step(2)
    lax.fori_loop(4, 8, near_step, 0)
    plane_total(0)
    mid_step(1)
    plane_total(1)
    far_step()
    plane_total(2)
    third_step(0)
    mid_to_y()
    plane_total(3)
    third_step(1)
    item_to_z()
    lax.fori_loop(4, 6, both_step, 0)
    mid_to_x()
    both_step(6, 0)
    column_step(6)
    item_total()
    mid_finish()
    plane_total(7)
    for part in (0, 1):
        for way in (0, 1):
            column_copy(part, 1, way).wait_recv()
            total[part, 1] += decode(column_in.at[part, 0, way], CHUNK)
    for k in (2, 1, 3):
        for part in (0, 1):
            encode(last_rows(part, k), last_out.at[part, k - 1])
            last_copy(part, k).start()
    item_to_share()
    halves = []
    for part in (0, 1):
        value = last_rows(part, 0)
        for k in (1, 2, 3):
            last_copy(part, k).wait_recv()
            value += decode(last_in.at[part, k - 1], EDGE_ROWS)
        halves.append(value)
    encode(jnp.concatenate(halves, axis=0), grads.at[q])
    for m in range(1, 8):
        grad_copy(m).start()
    item_share.wait_recv()
    item_last.start()

    def plane_drain(i, carry):
        for part in (0, 1):
            for way in (0, 1):
                half_copy(part, i, way).wait_send()
                near_copy(part, i, way).wait_send()
        return carry

    def peer_drain(o, carry):
        item_z_copy(o).wait_send()
        item_back(o).wait_send()
        mid_grad_copy(o).wait_send()
        return carry

    lax.fori_loop(0, 8, plane_drain, 0)
    lax.fori_loop(1, 8, peer_drain, 0)
    for way in (0, 1):
        mid_far_copy(way).wait_send()
        for part in (0, 1):
            far_copy(part, way).wait_send()
        for distance in (1, 2, 3):
            mid_copy(distance, way).wait_send()
            for part in (0, 1):
                column_copy(part, distance, way).wait_send()
    for k in (1, 2, 3):
        mid_y_copy(k).wait_send()
        mid_x_copy(k).wait_send()
        for part in (0, 1):
            last_copy(part, k).wait_send()
    item_last.wait_recv()

    def item_finish(n, carry):
        grad = decode(item_grads.at[n // 16, lax.rem(n // 8, 2), lax.rem(n, 8)], 32)
        rows = pl.ds(pl.multiple_of(n * 32, 32), 32)
        now = own_items[rows].astype(jnp.float32)
        new_items[rows] = now - item_step * (grad + shrinkage * now)
        return carry

    lax.fori_loop(0, 32, item_finish, 0)
    for m in range(1, 8):
        mid_grad_copy(m).wait_recv()
    for m in range(1, 8):
        grad_copy(m).wait_recv()

    def user_finish(j, carry):
        grad = jnp.concatenate(
            [decode(grads.at[j], 2 * EDGE_ROWS), decode(mid_grads.at[j], MIDDLE_ROWS)], axis=0
        )
        rows = pl.ds(pl.multiple_of(j * 128, 128), 128)
        now = own_users[rows].astype(jnp.float32)
        new_users[rows] = now - user_step * (grad + shrinkage * now)
        return carry

    lax.fori_loop(0, 8, user_finish, 0)
    for m in range(1, 8):
        grad_copy(m).wait_send()
    for early in (item_first, item_pair, item_share, item_last):
        early.wait_send()


def reduce(sums, item_sums, own_users, own_items):
    vmem = pl.BlockSpec(memory_space=pltpu.VMEM)
    dma = pltpu.SemaphoreType.DMA
    i16, f32 = jnp.int16, jnp.float32
    half = (2, 8, 2, coded_rows(CHUNK // 2), 128)
    near = (2, 8, 2, coded_rows(CHUNK), 128)
    far = (2, 2, coded_rows(CHUNK // 2), 128)
    column = (2, 3, 2, coded_rows(CHUNK), 128)
    last = (2, 3, coded_rows(EDGE_ROWS), 128)
    mid_far = (2, coded_rows(8 * MIDDLE_ROWS), 128)
    mid = (3, 2, coded_rows(16 * MIDDLE_ROWS), 128)
    mid_y = (3, coded_rows(4 * MIDDLE_ROWS), 128)
    mid_x = (3, coded_rows(MIDDLE_ROWS), 128)
    item_z = (7, coded_rows(32), 128)
    item_pair = (coded_rows(256), 128)
    both = lambda shape: [pltpu.VMEM(shape, i16)] * 2
    sems = lambda *shape: [dma(shape)] * 2
    return pl.pallas_call(
        reduce_kernel,
        out_shape=(
            jax.ShapeDtypeStruct((1024, 128), f32),
            jax.ShapeDtypeStruct((1024, 128), f32),
        ),
        in_specs=[vmem, vmem, vmem, vmem],
        out_specs=(vmem, vmem),
        scratch_shapes=[
            *both(half), *both(near), *both(far), *both(column),
            pltpu.VMEM((2, 2, CHUNK, 128), f32),
            *both(last),
            pltpu.VMEM((8, coded_rows(2 * EDGE_ROWS), 128), i16),
            *both(mid_far), *both(mid),
            pltpu.VMEM((16 * MIDDLE_ROWS, 128), f32),
            *both(mid_y),
            pltpu.VMEM((4 * MIDDLE_ROWS, 128), f32),
            *both(mid_x),
            pltpu.VMEM((8, coded_rows(MIDDLE_ROWS), 128), i16),
            pltpu.VMEM((4, 128, 128), f32), pltpu.VMEM((512, 128), f32),
            *both(item_pair),
            pltpu.VMEM((256, 128), f32),
            *both(item_z),
            pltpu.VMEM((2, 2, 8, coded_rows(32), 128), i16),
            *sems(2, 8, 2), *sems(2, 8, 2), *sems(2, 2), *sems(2, 3, 2),
            *sems(2, 3), *sems(7),
            *sems(2), *sems(3, 2), *sems(3), *sems(3), *sems(7),
            *sems(4), *sems(7), *sems(7),
        ],
        compiler_params=pltpu.CompilerParams(
            collective_id=1, has_side_effects=True, vmem_limit_bytes=16 * 2**20
        ),
    )(sums.reshape(8, 2, 2, 4, 128, 128), item_sums, own_users, own_items)


def body(user_factors, item_factors, block_user, block_item, live_blocks, ratings):
    slots = ratings.shape[2]
    scores = ratings.reshape(slots, 128, 128)
    lists = jnp.concatenate(
        [
            block_user.reshape(1, slots),
            block_item.reshape(1, slots),
            jnp.broadcast_to(live_blocks.reshape(1, 1), (1, slots)),
            jnp.zeros((5, slots), jnp.int32),
        ],
        axis=0,
    )
    users, all_scores, all_lists, no_users, no_items = gather(user_factors, scores, lists)
    core = lax.rem(lax.axis_index("user"), 2).astype(jnp.int32).reshape(1)
    user_sums, item_sums = local(
        core, all_lists, users.reshape(128, 128, 128), item_factors.reshape(8, 128, 128),
        all_scores.reshape(256, 128, 128), no_users, no_items,
    )
    return reduce(user_sums, item_sums, user_factors, item_factors)


def solution(mesh):
    return jax.shard_map(
        body,
        mesh=mesh,
        in_specs=(
            P("user", None),
            P("item", None),
            P("user", "item", None),
            P("user", "item", None),
            P("user", "item"),
            P("user", "item", None, None, None),
        ),
        out_specs=(P("user", None), P("item", None)),
        check_vma=False,
    )
```
